32 devices in a mesh: lat: 4 (over y, x), lon: 8 (over z, core).
Axes of the slice: x: 2, y: 2, z: 4, core: 2. Of those that a mesh axis runs over, the one named last changes fastest.
Arguments:
- tokens: bfloat16 [48, 384, 512], P('lat', 'lon'), may hold values from -6 to 6
- expert_ids: int32 [2, 4, 8, 576, 1], P(None, 'lat', 'lon'), may hold values from 0 to 15; in each aligned block of 576 rows (0 to 575, 576 to 1151, ..., all dimensions but the last counted through in order) at most 48 rows name the same one
- norm_gain: float32 [2, 2, 512], replicated, may hold values from 0.5 to 2
- weight_qkv: bfloat16 [2, 512, 1536], replicated, may hold values from -0.25 to 0.25
- weight_proj: bfloat16 [2, 512, 512], replicated, may hold values from -0.25 to 0.25
- temper: float32 [2, 16], replicated, may hold values from 0.5 to 12
- router: bfloat16 [2, 512, 16], replicated, may hold values from -0.25 to 0.25
- weight_in: bfloat16 [2, 32, 512, 1024], P(None, 'lon'), may hold values from -0.25 to 0.25
- weight_out: bfloat16 [2, 32, 1024, 512], P(None, 'lon'), may hold values from -0.125 to 0.125
Outputs:
- result: bfloat16 [48, 384, 512], P('lat', 'lon')
The draws below stay inside these ranges and needn't reach their ends.
Inputs may be any that keep to these rules, and one draw needn't show every extreme that they name: `expert_ids`: in each layer, among the 576 cells of one device's tile no expert is named more than 48 times.
All inputs are finite; a program needn't handle non-finite values.
Results may differ from the reference program's by a relative error of at most 0.028.
The reference program's roundings to bfloat16 on the way count: a program that leaves them out, or rounds other values in their place, can miss the bound.
Values may be sent and summed in bfloat16 or wider, within the bound.
No kernel may reach another device: no remote copies, remote signals or barrier semaphores. Data moves between devices by JAX's collectives and lax.ppermute only.
A program may use at most 128 MiB of HBM per device.

```python
import math
import jax
import jax.numpy as jnp
import numpy as np
from jax import lax

D = 512
HEADS = 16
WIN = 12
EXPERTS = 16
FF = 2048
LAYERS = 2
ROWS_DEV = 12
COLS_DEV = 48
TOK_DEV = 576
CAP = 48
BANDS = 4
SECTORS = 8
NLAT = 48
NLON = 384


def draw_temper(key, part):
    uniform_draw = jax.random.uniform(key, (LAYERS, HEADS), jnp.float32)
    lowest, highest = (0.5, 4.0)
    return jnp.exp(jnp.log(lowest) + uniform_draw * (jnp.log(highest) - jnp.log(lowest)))


def block_levels(stream_key, dims, split, least, high):
    gain, own = 1.0, jax.random.fold_in(stream_key, 6)
    for dim, shards_of in split:
        draws = jnp.exp(jax.random.uniform(jax.random.fold_in(own, dim), (shards_of,), jnp.float32, least / len(split), high / len(split)))
        gain = gain * jnp.repeat(draws, dims[dim] // shards_of).reshape([-1 if axis == dim else 1 for axis in range(len(dims))])
    return gain


def shared_out(stream_key, own, number, rows, count, top, most, slope):
    order = jax.random.permutation(stream_key, count)
    crowded, usual = load_shares(count, rows * top, most, slope, True), load_shares(count, rows * top, most, slope, False)
    places = jnp.arange(count)

    def named(tallies, offset_by):
        used = int((tallies > 0).sum())
        fixed = max(1, used // 4)
        moved = fixed + (places - fixed + offset_by * (used - fixed)) % max(1, count - fixed)
        return jnp.zeros((count,), jnp.int32).at[order[jnp.where(places < fixed, places, moved)]].set(jnp.asarray(tallies, jnp.int32))

    tallies = jnp.where(number % 4 == 0, named(crowded, number // 4), named(usual, number - number // 4 - 1))
    mixed = jax.random.permutation(jax.random.fold_in(own, 3), count)
    giver, taker = mixed[0:count // 2 * 2:2], mixed[1:count // 2 * 2:2]
    margin = jnp.minimum(tallies[giver] - 1, most - tallies[taker]) // 2
    margin = jnp.where((giver == order[0]) | (taker == order[0]) | (tallies[taker] == 0), 0, jnp.maximum(margin, 0))
    moved = jax.random.randint(jax.random.fold_in(own, 4), (count // 2,), 0, 1 << 20) % (margin + 1)
    tallies = tallies.at[giver].add(-moved).at[taker].add(moved)
    labels = jnp.searchsorted(jnp.cumsum(tallies), jnp.arange(rows * top), side="right").astype(jnp.int32)
    grid = labels.reshape(top, rows).T
    grid = grid[jax.random.permutation(jax.random.fold_in(own, 1), rows)]
    offset_by = jax.random.randint(jax.random.fold_in(own, 2), (rows, 1), 0, top)
    return jnp.take_along_axis(grid, (jnp.arange(top)[None, :] + offset_by) % top, axis=1)


def load_shares(count, total, most, slope, full):
    weights = [(1 << 20) // math.isqrt(rank ** slope) + 1 for rank in range(1, count + 1)]
    largest = most if full else min(most, max(-(-total // count), total * weights[0] // sum(weights)))
    least = 1 if total - largest >= count - 1 else 0
    holding, surplus = [largest] + [least] * (count - 1), total - largest - least * (count - 1)
    while surplus > 0:
        movable = [i for i in range(1, count) if holding[i] < largest] or [i for i in range(1, count) if holding[i] < most]
        whole, budget = sum([weights[i] for i in movable]), surplus
        for i in movable:
            addition = min(most - holding[i], max(1, budget * weights[i] // whole), surplus)
            holding[i] = holding[i] + addition
            surplus = surplus - addition
    return np.array(holding)


def bell_draw(key, shape, scale, reach, cuts=(), kind=jnp.bfloat16):
    result = scale * jax.random.normal(key, shape, jnp.float32)
    if cuts:
        result = result * block_levels(key, shape, cuts, -0.22, 0.18)
    return jnp.clip(result, -reach, reach).astype(kind)


def setup_inputs(seed: int = 0) -> dict:
    key_of = jax.random.split(jax.random.key(seed), 10)
    tokens = bell_draw(key_of[0], (NLAT, NLON, D), 1.0, 6.0, ((0, 4), (1, 8)))
    expert_ids_keys = jax.random.split(jax.random.fold_in(key_of[1], 1), LAYERS * BANDS * SECTORS * TOK_DEV // TOK_DEV)
    expert_ids_turns = jax.random.permutation(jax.random.fold_in(key_of[1], 3), LAYERS * BANDS * SECTORS * TOK_DEV // TOK_DEV)
    expert_ids = jax.vmap(lambda own, number: shared_out(jax.random.fold_in(key_of[1], 2), own, number, TOK_DEV, EXPERTS, 1, CAP, 2))(expert_ids_keys, expert_ids_turns).reshape((LAYERS, BANDS, SECTORS, TOK_DEV, 1))
    norm_gain = jnp.clip(jnp.exp(jax.random.uniform(key_of[2], (LAYERS, 2, D), jnp.float32, math.log(0.5), math.log(2.0))), 0.5, 2.0)
    weight_qkv = bell_draw(key_of[3], (LAYERS, D, 3 * D), D ** -0.5, 0.25)
    weight_proj = bell_draw(key_of[4], (LAYERS, D, D), D ** -0.5, 0.25)
    temper = draw_temper(jax.random.fold_in(key_of[9], 71), 0)
    router = bell_draw(key_of[6], (LAYERS, D, EXPERTS), D ** -0.5, 0.25)
    weight_in = bell_draw(key_of[7], (LAYERS, 2 * EXPERTS, D, FF // 2), D ** -0.5, 0.25, ((1, 8),))
    weight_out = bell_draw(key_of[8], (LAYERS, 2 * EXPERTS, FF // 2, D), FF ** -0.5, 0.125, ((1, 8),))
    return dict(tokens=tokens, expert_ids=expert_ids, norm_gain=norm_gain, weight_qkv=weight_qkv, weight_proj=weight_proj, temper=temper, router=router, weight_in=weight_in, weight_out=weight_out)


EPSILON = 1e-05

def layer_norm(values, gain_row):
    widened = values.astype(jnp.float32)
    centered = widened - lax.optimization_barrier(jnp.mean(widened, axis=-1, keepdims=True))
    variance = lax.optimization_barrier(jnp.mean(centered * centered, axis=-1, keepdims=True))
    return (centered * lax.rsqrt(variance + EPSILON) * gain_row).astype(jnp.bfloat16)

def to_windows(frame, window):
    height, breadth, channels = frame.shape
    pieces = frame.reshape(height // window, window, breadth // window, window, channels)
    return pieces.transpose(0, 2, 1, 3, 4).reshape(-1, window * window, channels)

def from_windows(blocks, height, breadth, window):
    channels = blocks.shape[-1]
    pieces = blocks.reshape(height // window, breadth // window, window, window, channels)
    return pieces.transpose(0, 2, 1, 3, 4).reshape(height, breadth, channels)

def window_attention(normed, seam_side, weight_qkv, weight_proj, scales, use_seam):
    height, breadth, channels = normed.shape
    blocks = to_windows(normed, WIN)
    window_count, window_area = (blocks.shape[0], blocks.shape[1])
    head_width = channels // HEADS
    projected = jnp.dot(blocks.reshape(-1, channels), weight_qkv, preferred_element_type=jnp.float32)
    projected = projected.astype(jnp.bfloat16).reshape(window_count, window_area, 3, HEADS, head_width)
    queries = projected[:, :, 0].astype(jnp.float32)
    key_rows = projected[:, :, 1].astype(jnp.float32)
    value_rows = projected[:, :, 2].astype(jnp.float32)
    scores = jnp.einsum('wqhd,wkhd->whqk', queries, key_rows)
    scores = scores * (scales / math.sqrt(head_width))[None, :, None, None]
    if use_seam:
        window_sides = to_windows(seam_side[:, :, None], WIN)[:, :, 0]
        same_side = window_sides[:, None, :, None] == window_sides[:, None, None, :]
        scores = jnp.where(same_side, scores, -1e+30)
    row_peak = lax.optimization_barrier(jnp.max(scores, axis=-1, keepdims=True))
    weights = jnp.exp(scores - row_peak)
    shares = (weights / lax.optimization_barrier(jnp.sum(weights, axis=-1, keepdims=True))).astype(jnp.bfloat16)
    context = jnp.einsum('whqk,wkhd->wqhd', shares.astype(jnp.float32), value_rows)
    context = context.astype(jnp.bfloat16).reshape(-1, channels)
    output = jnp.dot(context, weight_proj, preferred_element_type=jnp.float32)
    return from_windows(output.reshape(window_count, window_area, channels), height, breadth, WIN)

def reference(tokens, expert_ids, norm_gain, weight_qkv, weight_proj, temper, router, weight_in, weight_out):
    nlat_here, nlon_here, channels = tokens.shape
    amount = WIN // 2
    band_count = nlat_here // WIN
    token_total = nlat_here * nlon_here
    bound = BANDS * SECTORS * CAP
    seam_rows = jnp.arange(nlat_here, dtype=jnp.int32) >= nlat_here - amount
    seam_grid = jnp.broadcast_to(seam_rows[:, None], (nlat_here, nlon_here))
    current = tokens
    for layer_index in range(LAYERS):
        shifted = layer_index % 2 == 1
        frame = jnp.roll(current, (-amount, -amount), (0, 1)) if shifted else current
        normed = layer_norm(frame, norm_gain[layer_index, 0])

        def band_attention(inputs, layer_index=layer_index, shifted=shifted):
            band, band_side = inputs
            return window_attention(band, band_side, weight_qkv[layer_index], weight_proj[layer_index], temper[layer_index], shifted)
        attended = lax.map(band_attention, (normed.reshape(band_count, WIN, nlon_here, channels), seam_grid.reshape(band_count, WIN, nlon_here)))
        attended = attended.reshape(nlat_here, nlon_here, channels)
        mixed_grid = (frame.astype(jnp.float32) + attended).astype(jnp.bfloat16)
        if shifted:
            mixed_grid = jnp.roll(mixed_grid, (amount, amount), (0, 1))
        flat_mixed = mixed_grid.reshape(token_total, channels)
        normed_rows = layer_norm(flat_mixed, norm_gain[layer_index, 1])
        routes = expert_ids[layer_index, :, :, :, 0].reshape(BANDS, SECTORS, ROWS_DEV, COLS_DEV)
        routes = routes.transpose(0, 2, 1, 3).reshape(token_total).astype(jnp.int32)
        chosen = (routes[:, None] == jnp.arange(EXPERTS, dtype=jnp.int32)[None, :]).astype(jnp.float32)
        logits = jnp.dot(normed_rows, router[layer_index], preferred_element_type=jnp.float32)
        gating = jax.nn.sigmoid(lax.optimization_barrier(jnp.sum(logits * chosen, axis=1)))
        full_in = weight_in[layer_index].reshape(EXPERTS, 2, channels, FF // 2)
        full_in = full_in.transpose(0, 2, 1, 3).reshape(EXPERTS, channels, FF)
        full_out = weight_out[layer_index].reshape(EXPERTS, FF, channels)

        def add_expert(total, inputs, routes=routes, normed_rows=normed_rows):
            expert_index, expert_in, expert_out = inputs
            member = routes == expert_index
            picked = jnp.nonzero(member, size=bound, fill_value=0)[0]
            live = jnp.arange(bound, dtype=jnp.int32) < jnp.sum(member.astype(jnp.int32))
            hidden = jax.nn.gelu(jnp.dot(normed_rows[picked], expert_in, preferred_element_type=jnp.float32))
            produced = jnp.dot(hidden.astype(jnp.bfloat16), expert_out, preferred_element_type=jnp.float32)
            produced = produced.astype(jnp.bfloat16).astype(jnp.float32)
            produced = jnp.where(live[:, None], produced, jnp.zeros_like(produced))
            return (total.at[picked].add(produced), None)
        combined, _unused = lax.scan(add_expert, jnp.zeros((token_total, channels), jnp.float32), (jnp.arange(EXPERTS, dtype=jnp.int32), full_in, full_out))
        current = (flat_mixed.astype(jnp.float32) + gating[:, None] * combined).astype(jnp.bfloat16)
        current = current.reshape(nlat_here, nlon_here, channels)
    return current
```

```python
import functools
import math

import jax
import jax.numpy as jnp
import numpy as np
from jax import lax
from jax.experimental import pallas as pl
from jax.experimental.pallas import tpu as pltpu
from jax.sharding import PartitionSpec as P

WIN = 12
HALF = WIN // 2
EXPERTS = 16
LAYERS = 2
CAP = 48
EPSILON = 1e-05
LANES = 128
MIB = 1 << 20

F32 = jnp.float32
BF16 = jnp.bfloat16


def norm_rows(values, gain_row):
    centered = values - jnp.mean(values, axis=-1, keepdims=True)
    variance = jnp.mean(centered * centered, axis=-1, keepdims=True)
    return (centered * lax.rsqrt(variance + EPSILON) * gain_row).astype(BF16)


def dot(left, right, dims=((1,), (0,))):
    return lax.dot_general(left, right, (dims, ((), ())), preferred_element_type=F32)


def one_hot_columns(column, count):
    spread = lax.broadcasted_iota(jnp.int32, (column.shape[0], count), 1)
    return jnp.where(spread == column, 1.0, 0.0).astype(BF16)


def one_hot_rows(row, count):
    spread = lax.broadcasted_iota(jnp.int32, (count, row.shape[1]), 0)
    return jnp.where(spread == row, 1.0, 0.0).astype(BF16)


def route(ynorm, router, experts, target_row, gate_ref, piece_refs):
    logits = dot(ynorm, router)
    chosen = lax.broadcasted_iota(jnp.int32, logits.shape, 1) == experts
    picked = jnp.sum(jnp.where(chosen, logits, 0.0), axis=1, keepdims=True)
    gate_ref[...] = jax.nn.sigmoid(picked)
    slots = piece_refs[0].shape[0]
    for index, piece_ref in enumerate(piece_refs):
        spread = one_hot_rows(target_row - index * slots, slots)
        piece_ref[...] = dot(spread, ynorm).astype(BF16)


def attend(frame, layer, seam_ref, temper_ref, gain_ref, wqkv_ref, wproj_ref, qkv_ref, context_ref):
    total, channels = frame.shape
    heads = temper_ref.shape[1]
    width = channels // heads
    area = WIN * WIN
    windows = total // area
    group = LANES // width
    main = LANES
    rest = area - main
    lanes = group * area
    normed = norm_rows(frame, gain_ref[0, 0:1, :])
    qkv_ref[...] = dot(normed, wqkv_ref[0]).astype(BF16)

    lane = lax.broadcasted_iota(jnp.int32, (1, lanes), 1)
    leftover = lane >= group * main
    head_of = jnp.where(leftover, (lane - group * main) // rest, lane // main)
    query_of = jnp.where(leftover, main + (lane - group * main) % rest, lane % main)
    late = query_of >= area // 2
    seam = seam_ref[0, 0] > 0
    bias_early = jnp.where(jnp.logical_and(seam, late), -1e30, 0.0)
    bias_late = jnp.where(jnp.logical_and(seam, jnp.logical_not(late)), -1e30, 0.0)
    channel_head = lax.broadcasted_iota(jnp.int32, (1, LANES), 1) // width
    keep = [jnp.where(channel_head == h, 1.0, 0.0).astype(BF16) for h in range(group)]
    keep_f = [jnp.where(channel_head == h, 1.0, 0.0) for h in range(group)]

    def one_window(window):
        rows = pl.ds(window * area, area)
        for g in range(channels // LANES):
            q = qkv_ref[rows, g * LANES : (g + 1) * LANES]
            k = qkv_ref[rows, channels + g * LANES : channels + (g + 1) * LANES]
            v = qkv_ref[rows, 2 * channels + g * LANES : 2 * channels + (g + 1) * LANES]
            stacked = jnp.concatenate(
                [q[:main] * keep[h] for h in range(group)] + [q[main:] * keep[h] for h in range(group)], axis=0
            )
            scores = dot(k, stacked, ((1,), (1,)))
            scale = jnp.zeros((1, lanes), F32)
            for h in range(group):
                factor = temper_ref[layer, g * group + h] * (math.log2(math.e) / math.sqrt(width))
                scale = jnp.where(head_of == h, factor, scale)
            if layer % 2 == 1:
                scores = jnp.concatenate(
                    [scores[: area // 2] + bias_early, scores[area // 2 :] + bias_late], axis=0
                )
            peak = jnp.max(scores, axis=0, keepdims=True)
            weights = jnp.exp2((scores - peak) * scale)
            shares = (weights * (1.0 / jnp.sum(weights, axis=0, keepdims=True))).astype(BF16)
            mixed_t = dot(v, shares, ((0,), (0,)))
            picked = jnp.concatenate(
                [mixed_t[h * width : (h + 1) * width, h * main : (h + 1) * main] for h in range(group)], axis=0
            )
            first = jnp.transpose(picked)
            tail = jnp.transpose(mixed_t[:, group * main :])
            second = tail[:rest] * keep_f[0]
            for h in range(1, group):
                second = second + tail[h * rest : (h + 1) * rest] * keep_f[h]
            context = jnp.concatenate([first, second], axis=0).astype(BF16)
            context_ref[rows, g * LANES : (g + 1) * LANES] = context

    for window in range(windows):
        one_window(window)
    attended = dot(context_ref[...], wproj_ref[0])
    return (frame + attended).astype(BF16)


def first_kernel(
    seam_ref, temper_ref, tokens_ref, order_ref, experts_ref, target_ref, gain_ref, wqkv_ref, wproj_ref, router_ref,
    mixed_ref, gate_ref, *refs, layer
):
    *piece_refs, qkv_ref, context_ref = refs
    tokens = tokens_ref[...]
    frame = dot(one_hot_columns(order_ref[...], tokens.shape[0]), tokens)
    mixed = attend(frame, layer, seam_ref, temper_ref, gain_ref, wqkv_ref, wproj_ref, qkv_ref, context_ref)
    mixed_ref[...] = mixed
    ynorm = norm_rows(mixed.astype(F32), gain_ref[0, 1:2, :])
    route(ynorm, router_ref[0], experts_ref[...], target_ref[...], gate_ref, piece_refs)


def shifted_kernel(
    seam_ref, temper_ref, own_ref, north_ref, east_ref, corner_ref, gain_ref, wqkv_ref, wproj_ref,
    low_ref, high_ref, low_edge_ref, high_edge_ref, low_scratch, high_scratch, qkv_ref, context_ref, *, layer
):
    half, channels = own_ref.shape
    strip = HALF * HALF
    part = WIN * HALF
    edge = east_ref.shape[0]
    low_scratch[0:half] = own_ref[...].astype(F32)
    low_scratch[half : half + edge] = east_ref[...].astype(F32)
    high_scratch[0:half] = north_ref[...].astype(F32)
    high_scratch[half : half + edge] = corner_ref[...].astype(F32)
    pieces = []
    for window in range(half // part):
        start = strip + window * part
        pieces += [low_scratch[start : start + part], high_scratch[start : start + part]]
    frame = jnp.concatenate(pieces, axis=0)
    mixed = attend(frame, layer, seam_ref, temper_ref, gain_ref, wqkv_ref, wproj_ref, qkv_ref, context_ref)
    mixed = mixed.astype(F32)
    low, high = split_halves(mixed)
    low_ref[...] = low.astype(BF16)
    high_ref[...] = high.astype(BF16)
    low_edge_ref[...] = low[half - edge :].astype(BF16)
    high_edge_ref[...] = high[half - edge :].astype(BF16)


def split_halves(rows):
    part = WIN * HALF
    pieces = [rows[start : start + part] for start in range(0, rows.shape[0], part)]
    return jnp.concatenate(pieces[0::2], axis=0), jnp.concatenate(pieces[1::2], axis=0)


def route_kernel(own_ref, south_ref, west_ref, corner_ref, experts_ref, target_ref, gain_ref, router_ref,
                 rows_ref, gate_ref, *piece_refs):
    mixed = jnp.concatenate([own_ref[...], south_ref[...], west_ref[...], corner_ref[...]], axis=0)
    rows_ref[...] = mixed
    ynorm = norm_rows(mixed.astype(F32), gain_ref[0, 1:2, :])
    route(ynorm, router_ref[0], experts_ref[...], target_ref[...], gate_ref, piece_refs)


def expert_kernel(*refs, sources, steps, local):
    piece_refs = refs[:sources]
    own_in, own_out, far_in, far_out = refs[sources : sources + 4]
    out_refs = refs[sources + 4 : 2 * sources + 4]
    total_ref = refs[-1]
    step = pl.program_id(0)
    slots, channels = piece_refs[0].shape
    groups = slots // CAP
    mine = step // (steps // max(1, local // 2)) if local > 1 else 0
    other = mine + groups // 2 if local > 1 else 0

    @pl.when(step == 0)
    def _():
        total_ref[...] = jnp.zeros_like(total_ref)

    for place, first_ref, second_ref in ((mine, own_in, own_out), (other, far_in, far_out)):
        start = place * CAP
        if local > 1:
            start = pl.multiple_of(start, CAP)
        rows = jnp.concatenate([ref[pl.ds(start, CAP), :] for ref in piece_refs], axis=0)
        hidden = jax.nn.gelu(dot(rows, first_ref[0, 0])).astype(BF16)
        total_ref[place] += dot(hidden, second_ref[0, 0])

    @pl.when(step == steps - 1)
    def _():
        for index, ref in enumerate(out_refs):
            for g in range(groups):
                ref[g * CAP : (g + 1) * CAP, :] = total_ref[g, index * CAP : (index + 1) * CAP].astype(BF16)


def gathered_state(mixed_ref, gate_ref, target_ref, piece_refs):
    produced = jnp.concatenate([ref[...] for ref in piece_refs], axis=0)
    spread = one_hot_columns(target_ref[...], produced.shape[0])
    combined = dot(spread, produced)
    return (mixed_ref[...].astype(F32) + gate_ref[...] * combined).astype(BF16)


def combine_kernel(mixed_ref, gate_ref, target_ref, *refs):
    *piece_refs, north_ref, own_ref, corner_ref, east_ref = refs
    state = gathered_state(mixed_ref, gate_ref, target_ref, piece_refs).astype(F32)
    low, high = split_halves(state)
    edge = east_ref.shape[0]
    north_ref[...] = low.astype(BF16)
    own_ref[...] = high.astype(BF16)
    corner_ref[...] = low[:edge].astype(BF16)
    east_ref[...] = high[:edge].astype(BF16)


def last_kernel(mixed_ref, gate_ref, target_ref, order_ref, *refs):
    *piece_refs, out_ref = refs
    state = gathered_state(mixed_ref, gate_ref, target_ref, piece_refs)
    out_ref[...] = dot(one_hot_rows(order_ref[...], out_ref.shape[0]), state).astype(BF16)


def whole(shape):
    return pl.BlockSpec(shape, lambda *_: (0,) * len(shape))


def of_layer(array, layer):
    rest = array.shape[1:]
    return pl.BlockSpec((1,) + rest, lambda *_: (layer,) + (0,) * len(rest))


SCALARS = pl.BlockSpec(memory_space=pltpu.SMEM)


def call(kernel, ins, outs, scratch=(), limit=40, flops=0):
    arrays = [array for array, _ in ins]
    size = sum(a.size * a.dtype.itemsize for a in arrays)
    return pl.pallas_call(
        kernel,
        grid=(1,),
        in_specs=[spec if spec is not None else whole(array.shape) for array, spec in ins],
        out_specs=[whole(o.shape) for o in outs],
        out_shape=outs,
        scratch_shapes=list(scratch),
        compiler_params=pltpu.CompilerParams(vmem_limit_bytes=limit * MIB),
        cost_estimate=pl.CostEstimate(flops=flops, bytes_accessed=size, transcendentals=0),
    )(*arrays)


def run_experts(pieces, own_in, own_out, far_in, far_out, layer):
    sources = len(pieces)
    slots, channels = pieces[0].shape
    local, units = own_in.shape[1], own_in.shape[3]
    split = 2
    steps = local * split
    block = units // split
    first = pl.BlockSpec((1, 1, channels, block), lambda i: (layer, i // split, 0, i % split))
    second = pl.BlockSpec((1, 1, block, channels), lambda i: (layer, i // split, i % split, 0))
    groups = slots // CAP
    return pl.pallas_call(
        functools.partial(expert_kernel, sources=sources, steps=steps, local=local),
        grid=(steps,),
        in_specs=[whole(p.shape) for p in pieces] + [first, second, first, second],
        out_specs=[whole(p.shape) for p in pieces],
        out_shape=[jax.ShapeDtypeStruct(p.shape, BF16) for p in pieces],
        scratch_shapes=[pltpu.VMEM((groups, sources * CAP, channels), F32)],
        compiler_params=pltpu.CompilerParams(vmem_limit_bytes=24 * MIB),
        cost_estimate=pl.CostEstimate(
            flops=sources * slots * 8 * channels * units, bytes_accessed=4 * local * channels * units * 2,
            transcendentals=0
        ),
    )(*pieces, own_in, own_out, far_in, far_out)


def lat_lon_pairs(lat_step, lon_step):
    bands, sectors = lax.axis_size("lat"), lax.axis_size("lon")
    pairs = []
    for i in range(bands):
        for j in range(sectors):
            target = (i + lat_step) % bands * sectors + (j + lon_step) % sectors
            pairs.append((i * sectors + j, target))
    return pairs


def shift(value, lat_step, lon_step):
    return lax.ppermute(value, ("lat", "lon"), lat_lon_pairs(lat_step, lon_step))


def between(value, distance):
    sectors = lax.axis_size("lon")
    return lax.ppermute(value, "lon", [(s, s ^ distance) for s in range(sectors)])


def exchange(pieces):
    return [pieces[0]] + [between(pieces[k], 2 * k) for k in range(1, len(pieces))]


def per_device(tokens, expert_ids, norm_gain, weight_qkv, weight_proj, temper, router, weight_in, weight_out):
    row_count, col_count, channels = tokens.shape
    token_count = row_count * col_count
    half = token_count // 2
    strip = HALF * HALF
    part = WIN * HALF
    edge = 48
    sectors = lax.axis_size("lon")
    local = weight_in.shape[1]
    pieces_count = sectors // 2
    pair_experts = EXPERTS // pieces_count
    slots = pair_experts * CAP
    lon = lax.axis_index("lon")
    lat = lax.axis_index("lat")

    far_in = between(weight_in, 1)
    far_out = between(weight_out, 1)

    ids = expert_ids[:, 0, 0, :, 0]
    same = ids[:, :, None] == ids[:, None, :]
    earlier = jnp.arange(token_count)[:, None] > jnp.arange(token_count)[None, :]
    place = jnp.sum(jnp.where(same & earlier, 1, 0), axis=2)
    piece = (ids // pair_experts) ^ (lon // 2)
    inner = (ids % pair_experts) ^ (lon % 2 * (pair_experts // 2))
    target = piece * slots + inner * CAP + place

    def blocks(values):
        cut = values.reshape(row_count // HALF, HALF, col_count // HALF, HALF)
        return cut.transpose(0, 2, 1, 3).reshape(row_count // HALF, half)

    def plain_order(values):
        return blocks(values).reshape(2, half // part, part).transpose(1, 0, 2).reshape(token_count)

    def split_order(values, void):
        low, high = blocks(values)
        gap = lambda n: jnp.full((n,), void, jnp.int32)
        return jnp.concatenate([
            high[strip:], gap(strip), low[strip:], gap(strip),
            gap(edge - strip), high[:strip], gap(edge - strip), low[:strip],
        ])

    positions = jnp.arange(token_count, dtype=jnp.int32)
    order0 = plain_order(positions)
    target0, experts0 = plain_order(target[0]), plain_order(ids[0])
    order1 = split_order(positions, -1)
    target1, experts1 = split_order(target[1], -1), split_order(ids[1], -1)
    rows1 = target1.shape[0]
    seam = jnp.where(lat == lax.axis_size("lat") - 1, 1, 0).astype(jnp.int32).reshape(1, 1)

    shape = jax.ShapeDtypeStruct
    piece_shapes = [shape((slots, channels), BF16)] * pieces_count
    attention_scratch = [pltpu.VMEM((token_count, 3 * channels), BF16), pltpu.VMEM((token_count, channels), BF16)]

    layer = 0
    mixed, gate, *pieces = call(
        functools.partial(first_kernel, layer=layer),
        [(seam, SCALARS), (temper, SCALARS), (tokens.reshape(token_count, channels), None),
         (order0[:, None], None), (experts0[:, None], None), (target0[None, :], None),
         (norm_gain, of_layer(norm_gain, layer)), (weight_qkv, of_layer(weight_qkv, layer)),
         (weight_proj, of_layer(weight_proj, layer)), (router, of_layer(router, layer))],
        [shape((token_count, channels), BF16), shape((token_count, 1), F32)] + piece_shapes,
        attention_scratch,
        flops=4_000_000_000,
    )
    produced = moe(pieces, weight_in, weight_out, far_in, far_out, layer)
    north, own, corner, east = call(
        combine_kernel,
        [(mixed, None), (gate, None), (target0[:, None], None)] + [(p, None) for p in produced],
        [shape((half, channels), BF16)] * 2 + [shape((edge, channels), BF16)] * 2,
        flops=1_000_000_000,
    )

    layer = 1
    north = shift(north, -1, 0)
    east = shift(east, 0, -1)
    corner = shift(corner, -1, -1)
    low, high, low_edge, high_edge = call(
        functools.partial(shifted_kernel, layer=layer),
        [(seam, SCALARS), (temper, SCALARS), (own, None), (north, None), (east, None), (corner, None),
         (norm_gain, of_layer(norm_gain, layer)), (weight_qkv, of_layer(weight_qkv, layer)),
         (weight_proj, of_layer(weight_proj, layer))],
        [shape((half, channels), BF16)] * 2 + [shape((edge, channels), BF16)] * 2,
        [pltpu.VMEM((half + edge, channels), F32)] * 2 + attention_scratch,
        flops=3_000_000_000,
    )
    high = shift(high, 1, 0)
    low_edge = shift(low_edge, 0, 1)
    high_edge = shift(high_edge, 1, 1)
    mixed, gate, *pieces = call(
        route_kernel,
        [(low, None), (high, None), (low_edge, None), (high_edge, None),
         (experts1[:, None], None), (target1[None, :], None),
         (norm_gain, of_layer(norm_gain, layer)), (router, of_layer(router, layer))],
        [shape((rows1, channels), BF16), shape((rows1, 1), F32)] + piece_shapes,
        flops=1_000_000_000,
    )
    produced = moe(pieces, weight_in, weight_out, far_in, far_out, layer)
    (out,) = call(
        last_kernel,
        [(mixed, None), (gate, None), (target1[:, None], None), (order1[None, :], None)]
        + [(p, None) for p in produced],
        [shape((token_count, channels), BF16)],
        flops=1_000_000_000,
    )
    return out.reshape(row_count, col_count, channels)


def moe(pieces, own_in, own_out, far_in, far_out, layer):
    arrived = exchange(pieces)
    if len(arrived) == 4:
        order = [[2], [3], [0, 1]]
    else:
        order = [[k] for k in range(len(arrived))]
    produced = [None] * len(arrived)
    for members in order:
        outs = run_experts([arrived[k] for k in members], own_in, own_out, far_in, far_out, layer)
        for k, value in zip(members, outs):
            produced[k] = value
    return exchange(produced)


def solution(mesh):
    in_specs = (
        P("lat", "lon", None),
        P(None, "lat", "lon", None, None),
        P(),
        P(),
        P(),
        P(),
        P(),
        P(None, "lon", None, None),
        P(None, "lon", None, None),
    )
    out_specs = P("lat", "lon", None)
    return jax.shard_map(per_device, mesh=mesh, in_specs=in_specs, out_specs=out_specs, check_vma=False)
```

```python
import functools
import math

import jax
import jax.numpy as jnp
import numpy as np
from jax import lax
from jax.experimental import pallas as pl
from jax.experimental.pallas import tpu as pltpu
from jax.sharding import PartitionSpec as P

WIN = 12
HALF = WIN // 2
EXPERTS = 16
LAYERS = 2
CAP = 48
EPSILON = 1e-05
LANES = 128
MIB = 1 << 20

F32 = jnp.float32
BF16 = jnp.bfloat16


def norm_rows(values, gain_row):
    centered = values - jnp.mean(values, axis=-1, keepdims=True)
    variance = jnp.mean(centered * centered, axis=-1, keepdims=True)
    return (centered * lax.rsqrt(variance + EPSILON) * gain_row).astype(BF16)


def dot(left, right, dims=((1,), (0,))):
    return lax.dot_general(left, right, (dims, ((), ())), preferred_element_type=F32)


def one_hot_columns(column, count):
    spread = lax.broadcasted_iota(jnp.int32, (column.shape[0], count), 1)
    return jnp.where(spread == column, 1.0, 0.0).astype(BF16)


def one_hot_rows(row, count):
    spread = lax.broadcasted_iota(jnp.int32, (count, row.shape[1]), 0)
    return jnp.where(spread == row, 1.0, 0.0).astype(BF16)


def route(ynorm, router, experts, target_row, gate_ref, piece_refs):
    logits = dot(ynorm, router, ((1,), (1,)))
    chosen = lax.broadcasted_iota(jnp.int32, logits.shape, 1) == experts
    picked = jnp.sum(jnp.where(chosen, logits, 0.0), axis=1, keepdims=True)
    gate_ref[...] = jax.nn.sigmoid(picked)
    slots = piece_refs[0].shape[0]
    for index, piece_ref in enumerate(piece_refs):
        spread = one_hot_rows(target_row - index * slots, slots)
        piece_ref[...] = dot(spread, ynorm).astype(BF16)


def attend(frame, layer, seam_ref, temper_ref, gain_ref, wqkv_ref, wproj_ref, qkv_ref, context_ref):
    total, channels = frame.shape
    heads = temper_ref.shape[1]
    width = channels // heads
    area = WIN * WIN
    windows = total // area
    group = LANES // width
    main = LANES
    rest = area - main
    lanes = group * area
    normed = norm_rows(frame, gain_ref[0, 0:1, :])
    qkv_ref[...] = dot(normed, wqkv_ref[0]).astype(BF16)

    lane = lax.broadcasted_iota(jnp.int32, (1, lanes), 1)
    leftover = lane >= group * main
    head_of = jnp.where(leftover, (lane - group * main) // rest, lane // main)
    query_of = jnp.where(leftover, main + (lane - group * main) % rest, lane % main)
    late = query_of >= area // 2
    seam = seam_ref[0, 0] > 0
    bias_early = jnp.where(jnp.logical_and(seam, late), -1e30, 0.0)
    bias_late = jnp.where(jnp.logical_and(seam, jnp.logical_not(late)), -1e30, 0.0)
    channel_head = lax.broadcasted_iota(jnp.int32, (1, LANES), 1) // width
    keep = [jnp.where(channel_head == h, 1.0, 0.0).astype(BF16) for h in range(group)]
    keep_f = [jnp.where(channel_head == h, 1.0, 0.0) for h in range(group)]

    def one_window(window):
        rows = pl.ds(window * area, area)
        for g in range(channels // LANES):
            q = qkv_ref[rows, g * LANES : (g + 1) * LANES]
            k = qkv_ref[rows, channels + g * LANES : channels + (g + 1) * LANES]
            v = qkv_ref[rows, 2 * channels + g * LANES : 2 * channels + (g + 1) * LANES]
            stacked = jnp.concatenate(
                [q[:main] * keep[h] for h in range(group)] + [q[main:] * keep[h] for h in range(group)], axis=0
            )
            scores = dot(k, stacked, ((1,), (1,)))
            scale = jnp.zeros((1, lanes), F32)
            for h in range(group):
                factor = temper_ref[layer, g * group + h] * (math.log2(math.e) / math.sqrt(width))
                scale = jnp.where(head_of == h, factor, scale)
            if layer % 2 == 1:
                scores = jnp.concatenate(
                    [scores[: area // 2] + bias_early, scores[area // 2 :] + bias_late], axis=0
                )
            peak = jnp.max(scores, axis=0, keepdims=True)
            weights = jnp.exp2((scores - peak) * scale)
            shares = (weights * (1.0 / jnp.sum(weights, axis=0, keepdims=True))).astype(BF16)
            mixed_t = dot(v, shares, ((0,), (0,)))
            picked = jnp.concatenate(
                [mixed_t[h * width : (h + 1) * width, h * main : (h + 1) * main] for h in range(group)], axis=0
            )
            first = jnp.transpose(picked)
            tail = jnp.transpose(mixed_t[:, group * main :])
            second = tail[:rest] * keep_f[0]
            for h in range(1, group):
                second = second + tail[h * rest : (h + 1) * rest] * keep_f[h]
            context = jnp.concatenate([first, second], axis=0).astype(BF16)
            context_ref[rows, g * LANES : (g + 1) * LANES] = context

    for window in range(windows):
        one_window(window)
    attended = dot(context_ref[...], wproj_ref[0])
    return (frame + attended).astype(BF16)


def first_kernel(
    seam_ref, temper_ref, tokens_ref, order_ref, experts_ref, target_ref, gain_ref, wqkv_ref, wproj_ref, router_ref,
    mixed_ref, gate_ref, *refs, layer
):
    *piece_refs, qkv_ref, context_ref = refs
    tokens = tokens_ref[...]
    frame = dot(one_hot_columns(order_ref[...], tokens.shape[0]), tokens)
    mixed = attend(frame, layer, seam_ref, temper_ref, gain_ref, wqkv_ref, wproj_ref, qkv_ref, context_ref)
    mixed_ref[...] = mixed
    ynorm = norm_rows(mixed.astype(F32), gain_ref[0, 1:2, :])
    route(ynorm, router_ref[0], experts_ref[...], target_ref[...], gate_ref, piece_refs)


def shifted_kernel(
    seam_ref, temper_ref, own_ref, north_ref, east_ref, corner_ref, gain_ref, wqkv_ref, wproj_ref,
    low_ref, high_ref, low_edge_ref, high_edge_ref, low_scratch, high_scratch, qkv_ref, context_ref, *, layer
):
    half, channels = own_ref.shape
    strip = HALF * HALF
    part = WIN * HALF
    edge = east_ref.shape[0]
    low_scratch[0:half] = own_ref[...].astype(F32)
    low_scratch[half : half + edge] = east_ref[...].astype(F32)
    high_scratch[0:half] = north_ref[...].astype(F32)
    high_scratch[half : half + edge] = corner_ref[...].astype(F32)
    pieces = []
    for window in range(half // part):
        start = strip + window * part
        pieces += [low_scratch[start : start + part], high_scratch[start : start + part]]
    frame = jnp.concatenate(pieces, axis=0)
    mixed = attend(frame, layer, seam_ref, temper_ref, gain_ref, wqkv_ref, wproj_ref, qkv_ref, context_ref)
    mixed = mixed.astype(F32)
    low, high = split_halves(mixed)
    low_ref[...] = low.astype(BF16)
    high_ref[...] = high.astype(BF16)
    low_edge_ref[...] = low[half - edge :].astype(BF16)
    high_edge_ref[...] = high[half - edge :].astype(BF16)


def split_halves(rows):
    part = WIN * HALF
    pieces = [rows[start : start + part] for start in range(0, rows.shape[0], part)]
    return jnp.concatenate(pieces[0::2], axis=0), jnp.concatenate(pieces[1::2], axis=0)


def route_kernel(own_ref, south_ref, west_ref, corner_ref, experts_ref, target_ref, gain_ref, router_ref,
                 rows_ref, gate_ref, *piece_refs):
    mixed = jnp.concatenate([own_ref[...], south_ref[...], west_ref[...], corner_ref[...]], axis=0)
    rows_ref[...] = mixed
    ynorm = norm_rows(mixed.astype(F32), gain_ref[0, 1:2, :])
    route(ynorm, router_ref[0], experts_ref[...], target_ref[...], gate_ref, piece_refs)


def expert_kernel(*refs, sources, plan, layer):
    piece_refs = refs[:sources]
    sets = (len(refs) - 2 * sources - 3) // 2
    weights = refs[sources : sources + 2 * sets]
    out_refs = refs[sources + 2 * sets : 2 * sources + 2 * sets]
    first_ref, second_ref, arrived = refs[-3:]
    copies = []
    for unit, (which, entry, _) in enumerate(plan):
        pair = []
        for side, target in enumerate((first_ref, second_ref)):
            copy = pltpu.make_async_copy(
                weights[2 * which + side].at[layer, entry], target.at[unit], arrived.at[side, unit]
            )
            copy.start()
            pair.append(copy)
        copies.append(pair)
    totals = {}
    last = {place: unit for unit, (_, _, place) in enumerate(plan)}
    for unit, (_, _, place) in enumerate(plan):
        block = slice(place * CAP, (place + 1) * CAP)
        rows = jnp.concatenate([ref[block, :] for ref in piece_refs], axis=0)
        copies[unit][0].wait()
        hidden = jax.nn.gelu(dot(rows, first_ref[unit])).astype(BF16)
        copies[unit][1].wait()
        part = dot(hidden, second_ref[unit])
        total = totals[place] + part if place in totals else part
        totals[place] = total
        if last[place] == unit:
            for index, ref in enumerate(out_refs):
                ref[block, :] = total[index * CAP : (index + 1) * CAP].astype(BF16)


def gathered_state(mixed_ref, gate_ref, target_ref, piece_refs):
    produced = jnp.concatenate([ref[...] for ref in piece_refs], axis=0)
    spread = one_hot_columns(target_ref[...], produced.shape[0])
    combined = dot(spread, produced)
    return (mixed_ref[...].astype(F32) + gate_ref[...] * combined).astype(BF16)


def combine_kernel(mixed_ref, gate_ref, target_ref, *refs):
    *piece_refs, north_ref, own_ref, corner_ref, east_ref = refs
    state = gathered_state(mixed_ref, gate_ref, target_ref, piece_refs).astype(F32)
    low, high = split_halves(state)
    edge = east_ref.shape[0]
    north_ref[...] = low.astype(BF16)
    own_ref[...] = high.astype(BF16)
    corner_ref[...] = low[:edge].astype(BF16)
    east_ref[...] = high[:edge].astype(BF16)


def last_kernel(mixed_ref, gate_ref, target_ref, order_ref, *refs):
    *piece_refs, out_ref = refs
    state = gathered_state(mixed_ref, gate_ref, target_ref, piece_refs)
    out_ref[...] = dot(one_hot_rows(order_ref[...], out_ref.shape[0]), state).astype(BF16)


def whole(shape):
    return pl.BlockSpec(shape, lambda *_: (0,) * len(shape))


def of_layer(array, layer):
    rest = array.shape[1:]
    return pl.BlockSpec((1,) + rest, lambda *_: (layer,) + (0,) * len(rest))


SCALARS = pl.BlockSpec(memory_space=pltpu.SMEM)


def call(kernel, ins, outs, scratch=(), limit=60, flops=0):
    arrays = [array for array, _ in ins]
    size = sum(a.size * a.dtype.itemsize for a in arrays)
    return pl.pallas_call(
        kernel,
        grid=(1,),
        in_specs=[spec if spec is not None else whole(array.shape) for array, spec in ins],
        out_specs=[whole(o.shape) for o in outs],
        out_shape=outs,
        scratch_shapes=list(scratch),
        compiler_params=pltpu.CompilerParams(vmem_limit_bytes=limit * MIB),
        cost_estimate=pl.CostEstimate(flops=flops, bytes_accessed=size, transcendentals=0),
    )(*arrays)


def run_experts(pieces, weights, plan, layer):
    sources = len(pieces)
    slots, channels = pieces[0].shape
    units = weights[0][0].shape[3]
    flat = [array for pair in weights for array in pair]
    return pl.pallas_call(
        functools.partial(expert_kernel, sources=sources, plan=plan, layer=layer),
        grid=(1,),
        in_specs=[whole(p.shape) for p in pieces] + [pl.BlockSpec(memory_space=pltpu.HBM)] * len(flat),
        out_specs=[whole(p.shape) for p in pieces],
        out_shape=[jax.ShapeDtypeStruct(p.shape, BF16) for p in pieces],
        scratch_shapes=[
            pltpu.VMEM((len(plan), channels, units), BF16),
            pltpu.VMEM((len(plan), units, channels), BF16),
            pltpu.SemaphoreType.DMA((2, len(plan))),
        ],
        compiler_params=pltpu.CompilerParams(vmem_limit_bytes=60 * MIB),
        cost_estimate=pl.CostEstimate(
            flops=len(plan) * 4 * channels * units * 192,
            bytes_accessed=len(plan) * 4 * channels * units,
            transcendentals=0,
        ),
    )(*pieces, *flat)


def lat_lon_pairs(lat_step, lon_step):
    bands, sectors = lax.axis_size("lat"), lax.axis_size("lon")
    pairs = []
    for i in range(bands):
        for j in range(sectors):
            target = (i + lat_step) % bands * sectors + (j + lon_step) % sectors
            pairs.append((i * sectors + j, target))
    return pairs


def shift(value, lat_step, lon_step):
    return lax.ppermute(value, ("lat", "lon"), lat_lon_pairs(lat_step, lon_step))


def between(value, distance):
    sectors = lax.axis_size("lon")
    return lax.ppermute(value, "lon", [(s, s ^ distance) for s in range(sectors)])


def per_device(tokens, expert_ids, norm_gain, weight_qkv, weight_proj, temper, router, weight_in, weight_out):
    row_count, col_count, channels = tokens.shape
    token_count = row_count * col_count
    half = token_count // 2
    strip = HALF * HALF
    part = WIN * HALF
    edge = 48
    sectors = lax.axis_size("lon")
    local = weight_in.shape[1]
    pieces_count = sectors // 2
    pair_experts = EXPERTS // pieces_count
    slots = pair_experts * CAP
    chunks = 2 if local > 1 else 1
    lon = lax.axis_index("lon")
    lat = lax.axis_index("lat")

    far_in = between(weight_in, 1)
    far_out = between(weight_out, 1)

    router = router.transpose(0, 2, 1)

    ids = expert_ids[:, 0, 0, :, 0]
    same = ids[:, :, None] == ids[:, None, :]
    earlier = jnp.arange(token_count)[:, None] > jnp.arange(token_count)[None, :]
    place = jnp.sum(jnp.where(same & earlier, 1, 0), axis=2)
    piece = (ids // pair_experts) ^ (lon // 2)
    inner = (ids % pair_experts) ^ (lon % 2 * (pair_experts // 2))
    target = piece * slots + inner * CAP + place

    def blocks(values):
        cut = values.reshape(row_count // HALF, HALF, col_count // HALF, HALF)
        return cut.transpose(0, 2, 1, 3).reshape(row_count // HALF, half)

    def plain_order(values):
        return blocks(values).reshape(2, half // part, part).transpose(1, 0, 2).reshape(token_count)

    def split_order(values, void):
        low, high = blocks(values)
        gap = lambda n: jnp.full((n,), void, jnp.int32)
        return jnp.concatenate([
            high[strip:], gap(strip), low[strip:], gap(strip),
            gap(edge - strip), high[:strip], gap(edge - strip), low[:strip],
        ])

    positions = jnp.arange(token_count, dtype=jnp.int32)
    order0 = plain_order(positions)
    target0, experts0 = plain_order(target[0]), plain_order(ids[0])
    order1 = split_order(positions, -1)
    target1, experts1 = split_order(target[1], -1), split_order(ids[1], -1)
    rows1 = target1.shape[0]
    seam = jnp.where(lat == lax.axis_size("lat") - 1, 1, 0).astype(jnp.int32).reshape(1, 1)

    shape = jax.ShapeDtypeStruct
    piece_shapes = [shape((slots // chunks, channels), BF16)] * (pieces_count * chunks)
    attention_scratch = [pltpu.VMEM((token_count, 3 * channels), BF16), pltpu.VMEM((token_count, channels), BF16)]

    layer = 0
    mixed, gate, *pieces = call(
        functools.partial(first_kernel, layer=layer),
        [(seam, SCALARS), (temper, SCALARS), (tokens.reshape(token_count, channels), None),
         (order0[:, None], None), (experts0[:, None], None), (target0[None, :], None),
         (norm_gain, of_layer(norm_gain, layer)), (weight_qkv, of_layer(weight_qkv, layer)),
         (weight_proj, of_layer(weight_proj, layer)), (router, of_layer(router, layer))],
        [shape((token_count, channels), BF16), shape((token_count, 1), F32)] + piece_shapes,
        attention_scratch,
        flops=4_000_000_000,
    )
    pieces = [pieces[k * chunks : (k + 1) * chunks] for k in range(pieces_count)]
    produced = moe(pieces, (weight_in, weight_out), (far_in, far_out), local, layer)
    north, own, corner, east = call(
        combine_kernel,
        [(mixed, None), (gate, None), (target0[:, None], None)] + [(p, None) for p in produced],
        [shape((half, channels), BF16)] * 2 + [shape((edge, channels), BF16)] * 2,
        flops=1_000_000_000,
    )

    layer = 1
    north = shift(north, -1, 0)
    east = shift(east, 0, -1)
    corner = shift(corner, -1, -1)
    low, high, low_edge, high_edge = call(
        functools.partial(shifted_kernel, layer=layer),
        [(seam, SCALARS), (temper, SCALARS), (own, None), (north, None), (east, None), (corner, None),
         (norm_gain, of_layer(norm_gain, layer)), (weight_qkv, of_layer(weight_qkv, layer)),
         (weight_proj, of_layer(weight_proj, layer))],
        [shape((half, channels), BF16)] * 2 + [shape((edge, channels), BF16)] * 2,
        [pltpu.VMEM((half + edge, channels), F32)] * 2 + attention_scratch,
        flops=3_000_000_000,
    )
    high = shift(high, 1, 0)
    low_edge = shift(low_edge, 0, 1)
    high_edge = shift(high_edge, 1, 1)
    mixed, gate, *pieces = call(
        route_kernel,
        [(low, None), (high, None), (low_edge, None), (high_edge, None),
         (experts1[:, None], None), (target1[None, :], None),
         (norm_gain, of_layer(norm_gain, layer)), (router, of_layer(router, layer))],
        [shape((rows1, channels), BF16), shape((rows1, 1), F32)] + piece_shapes,
        flops=1_000_000_000,
    )
    pieces = [pieces[k * chunks : (k + 1) * chunks] for k in range(pieces_count)]
    produced = moe(pieces, (weight_in, weight_out), (far_in, far_out), local, layer)
    (out,) = call(
        last_kernel,
        [(mixed, None), (gate, None), (target1[:, None], None), (order1[None, :], None)]
        + [(p, None) for p in produced],
        [shape((token_count, channels), BF16)],
        flops=1_000_000_000,
    )
    return out.reshape(row_count, col_count, channels)


def after(value, done):
    return lax.optimization_barrier((value, done))[0]


def moe(pieces, own, far, local, layer):
    if local > 1:
        plans = [
            ([own], [(0, entry, entry // 2) for entry in range(local)]),
            ([far], [(0, entry, entry // 2) for entry in range(local)]),
        ]
    else:
        plans = [([own, far], [(0, 0, 0), (1, 0, 0)])]
    count, chunks = len(pieces), len(plans)
    near = [k for k in range(count) if k < count // 2]
    away = [k for k in range(count) if k >= count // 2]
    back = [[None] * chunks for _ in range(count)]
    held = None
    arrived_near = [[between(pieces[k][c], 2 * k) if k else pieces[k][c] for c in range(chunks)] for k in near]
    for c in range(chunks):
        sent = [pieces[k][c] for k in away]
        if held is not None:
            sent = [after(value, held) for value in sent]
        arrived = [between(value, 2 * k) for k, value in zip(away, sent)]
        outs = run_experts([arrived_near[i][c] for i in range(len(near))], *plans[c], layer)
        for k, value in zip(near, outs):
            back[k][c] = between(value, 2 * k) if k else value
        held = outs[0]
        outs = run_experts(arrived, *plans[c], layer)
        for k, value in zip(away, outs):
            back[k][c] = between(value, 2 * k)
    return [value for piece in back for value in piece]


def solution(mesh):
    in_specs = (
        P("lat", "lon", None),
        P(None, "lat", "lon", None, None),
        P(),
        P(),
        P(),
        P(),
        P(),
        P(None, "lon", None, None),
        P(None, "lon", None, None),
    )
    out_specs = P("lat", "lon", None)
    return jax.shard_map(per_device, mesh=mesh, in_specs=in_specs, out_specs=out_specs, check_vma=False)
```

```python
import functools
import math

import jax
import jax.numpy as jnp
import numpy as np
from jax import lax
from jax.experimental import pallas as pl
from jax.experimental.pallas import tpu as pltpu
from jax.sharding import PartitionSpec as P

WIN = 12
HALF = WIN // 2
EXPERTS = 16
LAYERS = 2
CAP = 48
EPSILON = 1e-05
LANES = 128
MIB = 1 << 20

F32 = jnp.float32
BF16 = jnp.bfloat16


def norm_rows(values, gain_row):
    centered = values - jnp.mean(values, axis=-1, keepdims=True)
    variance = jnp.mean(centered * centered, axis=-1, keepdims=True)
    return (centered * lax.rsqrt(variance + EPSILON) * gain_row).astype(BF16)


def dot(left, right, dims=((1,), (0,))):
    return lax.dot_general(left, right, (dims, ((), ())), preferred_element_type=F32)


def one_hot_columns(column, count):
    spread = lax.broadcasted_iota(jnp.int32, (column.shape[0], count), 1)
    return jnp.where(spread == column, 1.0, 0.0).astype(BF16)


def one_hot_rows(row, count):
    spread = lax.broadcasted_iota(jnp.int32, (count, row.shape[1]), 0)
    return jnp.where(spread == row, 1.0, 0.0).astype(BF16)


def slots_of(ids, order, place_ref, pair_experts):
    count = ids.shape[0]
    chosen = lax.broadcasted_iota(jnp.int32, (count, LANES), 1) == ids
    earlier = lax.broadcasted_iota(jnp.int32, (count, count), 0) > lax.broadcasted_iota(jnp.int32, (count, count), 1)
    before = dot(jnp.where(earlier, 1.0, 0.0).astype(BF16), jnp.where(chosen, 1.0, 0.0).astype(BF16))
    place = jnp.sum(jnp.where(chosen, before, 0.0), axis=1, keepdims=True).astype(jnp.int32)
    piece = lax.div(ids, pair_experts) ^ place_ref[0, 1]
    inner = lax.rem(ids, pair_experts) ^ (place_ref[0, 2] * (pair_experts // 2))
    target = (piece * pair_experts + inner) * CAP + place
    lane = lax.broadcasted_iota(jnp.int32, (count, LANES), 1)
    parts = jnp.where(lane == 0, target // 256, jnp.where(lane == 1, target % 256, jnp.where(lane == 2, ids, 1)))
    moved = dot(one_hot_columns(order, count), parts.astype(F32).astype(BF16))
    slot = jnp.where(moved[:, 3:4] > 0.5, moved[:, 0:1] * 256.0 + moved[:, 1:2], -1.0)
    row = jnp.transpose(jnp.broadcast_to(slot, (slot.shape[0], LANES)))[0:1, :]
    return moved[:, 2:3], slot, row


def route(ynorm, router, experts, target_row, piece_refs):
    logits = dot(ynorm, router, ((1,), (1,)))
    chosen = lax.broadcasted_iota(jnp.int32, logits.shape, 1) == experts.astype(jnp.int32)
    picked = jnp.sum(jnp.where(chosen, logits, 0.0), axis=1, keepdims=True)
    target = target_row.astype(jnp.int32)
    slots = piece_refs[0].shape[0]
    for index, piece_ref in enumerate(piece_refs):
        spread = one_hot_rows(target - index * slots, slots)
        piece_ref[...] = dot(spread, ynorm).astype(BF16)
    return jax.nn.sigmoid(picked)


def fetch(layer, sources, targets, arrived):
    copies = []
    for index, (source, target) in enumerate(zip(sources, targets)):
        copy = pltpu.make_async_copy(source.at[layer], target, arrived.at[index])
        copy.start()
        copies.append(copy)
    return copies


def attend(frame, layer, place_ref, temper_ref, gain_ref, wqkv_ref, wproj_ref, qkv_ref, context_ref, copies):
    total, channels = frame.shape
    heads = temper_ref.shape[1]
    width = channels // heads
    area = WIN * WIN
    windows = total // area
    group = LANES // width
    main = LANES
    rest = area - main
    lanes = group * area
    normed = norm_rows(frame, gain_ref[0, 0:1, :])
    copies[0].wait()
    qkv_ref[...] = dot(normed, wqkv_ref[...]).astype(BF16)

    lane = lax.broadcasted_iota(jnp.int32, (1, lanes), 1)
    leftover = lane >= group * main
    head_of = jnp.where(leftover, (lane - group * main) // rest, lane // main)
    query_of = jnp.where(leftover, main + (lane - group * main) % rest, lane % main)
    late = query_of >= area // 2
    seam = place_ref[0, 0] > 0
    bias_early = jnp.where(jnp.logical_and(seam, late), -1e30, 0.0)
    bias_late = jnp.where(jnp.logical_and(seam, jnp.logical_not(late)), -1e30, 0.0)
    channel_head = lax.broadcasted_iota(jnp.int32, (1, LANES), 1) // width
    keep = [jnp.where(channel_head == h, 1.0, 0.0).astype(BF16) for h in range(group)]
    keep_f = [jnp.where(channel_head == h, 1.0, 0.0) for h in range(group)]

    def one_window(window):
        rows = pl.ds(window * area, area)
        for g in range(channels // LANES):
            q = qkv_ref[rows, g * LANES : (g + 1) * LANES]
            k = qkv_ref[rows, channels + g * LANES : channels + (g + 1) * LANES]
            v = qkv_ref[rows, 2 * channels + g * LANES : 2 * channels + (g + 1) * LANES]
            stacked = jnp.concatenate(
                [q[:main] * keep[h] for h in range(group)] + [q[main:] * keep[h] for h in range(group)], axis=0
            )
            scores = dot(k, stacked, ((1,), (1,)))
            scale = jnp.zeros((1, lanes), F32)
            for h in range(group):
                factor = temper_ref[layer, g * group + h] * (math.log2(math.e) / math.sqrt(width))
                scale = jnp.where(head_of == h, factor, scale)
            if layer % 2 == 1:
                scores = jnp.concatenate(
                    [scores[: area // 2] + bias_early, scores[area // 2 :] + bias_late], axis=0
                )
            peak = jnp.max(scores, axis=0, keepdims=True)
            weights = jnp.exp2((scores - peak) * scale)
            shares = (weights * (1.0 / jnp.sum(weights, axis=0, keepdims=True))).astype(BF16)
            mixed_t = dot(v, shares, ((0,), (0,)))
            picked = jnp.concatenate(
                [mixed_t[h * width : (h + 1) * width, h * main : (h + 1) * main] for h in range(group)], axis=0
            )
            first = jnp.transpose(picked)
            tail = jnp.transpose(mixed_t[:, group * main :])
            second = tail[:rest] * keep_f[0]
            for h in range(1, group):
                second = second + tail[h * rest : (h + 1) * rest] * keep_f[h]
            context = jnp.concatenate([first, second], axis=0).astype(BF16)
            context_ref[rows, g * LANES : (g + 1) * LANES] = context

    for window in range(windows):
        one_window(window)
    copies[1].wait()
    attended = dot(context_ref[...], wproj_ref[...])
    return (frame + attended).astype(BF16)


def first_kernel(
    place_ref, temper_ref, tokens_ref, order_ref, ids_ref, gain_ref, wqkv_hbm, wproj_hbm, router_ref,
    mixed_ref, info_ref, *refs, layer, pair_experts
):
    *piece_refs, wqkv_ref, wproj_ref, qkv_ref, context_ref, arrived = refs
    copies = fetch(layer, (wqkv_hbm, wproj_hbm), (wqkv_ref, wproj_ref), arrived)
    tokens = tokens_ref[...]
    frame = dot(one_hot_columns(order_ref[...], tokens.shape[0]), tokens)
    mixed = attend(frame, layer, place_ref, temper_ref, gain_ref, wqkv_ref, wproj_ref, qkv_ref, context_ref, copies)
    mixed_ref[...] = mixed
    ynorm = norm_rows(mixed.astype(F32), gain_ref[0, 1:2, :])
    experts, slot, slot_row = slots_of(ids_ref[0], order_ref[...], place_ref, pair_experts)
    gate = route(ynorm, router_ref[0], experts, slot_row, piece_refs)
    info_ref[...] = jnp.concatenate([gate, slot], axis=1)


def slots_kernel(place_ref, ids_ref, order_ref, _, columns_ref, row_ref, *, pair_experts):
    experts, slot, slot_row = slots_of(ids_ref[0], order_ref[...], place_ref, pair_experts)
    columns_ref[...] = jnp.concatenate([experts, slot], axis=1)
    row_ref[...] = slot_row


def shifted_kernel(
    place_ref, temper_ref, own_ref, north_ref, east_ref, corner_ref, gain_ref, wqkv_hbm, wproj_hbm,
    low_ref, high_ref, low_edge_ref, high_edge_ref,
    low_scratch, high_scratch, wqkv_ref, wproj_ref, qkv_ref, context_ref, arrived, *, layer
):
    copies = fetch(layer, (wqkv_hbm, wproj_hbm), (wqkv_ref, wproj_ref), arrived)
    half, channels = own_ref.shape
    strip = HALF * HALF
    part = WIN * HALF
    edge = east_ref.shape[0]
    low_scratch[0:half] = own_ref[...].astype(F32)
    low_scratch[half : half + edge] = east_ref[...].astype(F32)
    high_scratch[0:half] = north_ref[...].astype(F32)
    high_scratch[half : half + edge] = corner_ref[...].astype(F32)
    pieces = []
    for window in range(half // part):
        start = strip + window * part
        pieces += [low_scratch[start : start + part], high_scratch[start : start + part]]
    frame = jnp.concatenate(pieces, axis=0)
    mixed = attend(frame, layer, place_ref, temper_ref, gain_ref, wqkv_ref, wproj_ref, qkv_ref, context_ref, copies)
    mixed = mixed.astype(F32)
    low, high = split_halves(mixed)
    low_ref[...] = low.astype(BF16)
    high_ref[...] = high.astype(BF16)
    low_edge_ref[...] = low[half - edge :].astype(BF16)
    high_edge_ref[...] = high[half - edge :].astype(BF16)


def split_halves(rows):
    part = WIN * HALF
    pieces = [rows[start : start + part] for start in range(0, rows.shape[0], part)]
    return jnp.concatenate(pieces[0::2], axis=0), jnp.concatenate(pieces[1::2], axis=0)


def route_kernel(own_ref, south_ref, west_ref, corner_ref, columns_ref, row_ref, gain_ref, router_ref,
                 rows_ref, info_ref, *piece_refs):
    mixed = jnp.concatenate([own_ref[...], south_ref[...], west_ref[...], corner_ref[...]], axis=0)
    rows_ref[...] = mixed
    ynorm = norm_rows(mixed.astype(F32), gain_ref[0, 1:2, :])
    gate = route(ynorm, router_ref[0], columns_ref[:, 0:1], row_ref[...], piece_refs)
    info_ref[...] = jnp.concatenate([gate, columns_ref[:, 1:2]], axis=1)


def expert_rows(piece_refs, out_refs, block, first, second, carried, last):
    rows = jnp.concatenate([ref[block, :] for ref in piece_refs], axis=0)
    hidden = jax.nn.gelu(dot(rows, first())).astype(BF16)
    part = dot(hidden, second())
    total = part if carried is None else carried + part
    if last:
        for index, ref in enumerate(out_refs):
            ref[block, :] = total[index * CAP : (index + 1) * CAP].astype(BF16)
    return total


def near_kernel(*refs, sources, plan, layer):
    piece_hbm = refs[:sources]
    weights = refs[sources : sources + 4]
    out_refs = refs[sources + 4 : 2 * sources + 4]
    first_ref, second_ref, piece_ref, arrived, here = refs[2 * sources + 4 :]
    moves = []
    for index, ref in enumerate(piece_hbm):
        move = pltpu.make_async_copy(ref, piece_ref.at[index], here.at[index])
        move.start()
        moves.append(move)
    copies = []
    for unit, (which, entry, _) in enumerate(plan):
        pair = []
        for side, target in enumerate((first_ref, second_ref)):
            copy = pltpu.make_async_copy(
                weights[2 * which + side].at[layer, entry], target.at[unit], arrived.at[side, unit]
            )
            copy.start()
            pair.append(copy)
        copies.append(pair)
    for move in moves:
        move.wait()
    totals = {}
    last = {place: unit for unit, (_, _, place) in enumerate(plan)}
    pieces = [piece_ref.at[index] for index in range(sources)]

    def wait_for(unit, side, ref):
        copies[unit][side].wait()
        return ref[unit]

    for unit, (_, _, place) in enumerate(plan):
        block = slice(place * CAP, (place + 1) * CAP)
        totals[place] = expert_rows(
            pieces, out_refs, block,
            functools.partial(wait_for, unit, 0, first_ref), functools.partial(wait_for, unit, 1, second_ref),
            totals.get(place), last[place] == unit,
        )


def away_kernel(*refs, sources, plan, base):
    piece_hbm = refs[:sources]
    first_ref, second_ref = refs[sources : sources + 2]
    out_refs = refs[sources + 2 : 2 * sources + 2]
    piece_ref, here = refs[2 * sources + 2 :]
    size = out_refs[0].shape[0]
    moves = []
    for index, ref in enumerate(piece_hbm):
        move = pltpu.make_async_copy(ref.at[pl.ds(base * CAP, size)], piece_ref.at[index], here.at[index])
        move.start()
        moves.append(move)
    for move in moves:
        move.wait()
    totals = {}
    last = {place: unit for unit, place in plan}
    pieces = [piece_ref.at[index] for index in range(sources)]
    for unit, place in plan:
        block = slice((place - base) * CAP, (place - base + 1) * CAP)
        totals[place] = expert_rows(
            pieces, out_refs, block, lambda unit=unit: first_ref[unit], lambda unit=unit: second_ref[unit],
            totals.get(place), last[place] == unit,
        )


def gathered_state(mixed_ref, info_ref, piece_refs):
    produced = jnp.concatenate([ref[...] for ref in piece_refs], axis=0)
    spread = one_hot_columns(info_ref[:, 1:2].astype(jnp.int32), produced.shape[0])
    combined = dot(spread, produced)
    return (mixed_ref[...].astype(F32) + info_ref[:, 0:1] * combined).astype(BF16)


def combine_kernel(mixed_ref, info_ref, *refs):
    *piece_refs, north_ref, own_ref, corner_ref, east_ref = refs
    state = gathered_state(mixed_ref, info_ref, piece_refs).astype(F32)
    low, high = split_halves(state)
    edge = east_ref.shape[0]
    north_ref[...] = low.astype(BF16)
    own_ref[...] = high.astype(BF16)
    corner_ref[...] = low[:edge].astype(BF16)
    east_ref[...] = high[:edge].astype(BF16)


def last_kernel(mixed_ref, info_ref, order_ref, *refs):
    *piece_refs, out_ref = refs
    state = gathered_state(mixed_ref, info_ref, piece_refs)
    out_ref[...] = dot(one_hot_rows(order_ref[...], out_ref.shape[0]), state).astype(BF16)


def whole(shape):
    return pl.BlockSpec(shape, lambda *_: (0,) * len(shape))


def of_layer(array, layer):
    rest = array.shape[1:]
    return pl.BlockSpec((1,) + rest, lambda *_: (layer,) + (0,) * len(rest))


SCALARS = pl.BlockSpec(memory_space=pltpu.SMEM)
IN_HBM = pl.BlockSpec(memory_space=pltpu.HBM)
IN_VMEM = pl.BlockSpec(memory_space=pltpu.VMEM)
SMALL = 1 << 14


def keep_out(array):
    if array.size < SMALL:
        return array
    return pltpu.with_memory_space_constraint(array, pltpu.HBM)


def call(kernel, ins, outs, scratch=(), limit=40, flops=0):
    arrays = [array for array, _ in ins]
    size = sum(a.size * a.dtype.itemsize for a in arrays)
    return pl.pallas_call(
        kernel,
        grid=(1,),
        in_specs=[spec if spec is not None else whole(array.shape) for array, spec in ins],
        out_specs=[whole(o.shape) for o in outs],
        out_shape=outs,
        scratch_shapes=list(scratch),
        compiler_params=pltpu.CompilerParams(vmem_limit_bytes=limit * MIB),
        cost_estimate=pl.CostEstimate(flops=flops, bytes_accessed=size, transcendentals=0),
    )(*[keep_out(array) if spec is not SCALARS else array for array, spec in ins])


def run_near(pieces, weights, plan, layer):
    sources = len(pieces)
    slots, channels = pieces[0].shape
    units = weights[0].shape[3]
    held = [pltpu.VMEM((len(plan), channels, units), BF16), pltpu.VMEM((len(plan), units, channels), BF16)]
    outs = pl.pallas_call(
        functools.partial(near_kernel, sources=sources, plan=plan, layer=layer),
        in_specs=[IN_HBM] * (sources + 4),
        out_specs=[IN_VMEM] * (sources + 2),
        out_shape=[jax.ShapeDtypeStruct(p.shape, BF16) for p in pieces] + held,
        scratch_shapes=[
            pltpu.VMEM((sources, slots, channels), BF16),
            pltpu.SemaphoreType.DMA((2, len(plan))),
            pltpu.SemaphoreType.DMA((sources,)),
        ],
        compiler_params=pltpu.CompilerParams(vmem_limit_bytes=24 * MIB),
        cost_estimate=pl.CostEstimate(
            flops=4_000_000_000, bytes_accessed=len(plan) * 4 * channels * units, transcendentals=0
        ),
    )(*[keep_out(p) for p in pieces], *[keep_out(w) for w in weights])
    return outs[:sources], outs[sources:]


def run_away(pieces, held, plan, layer):
    sources = len(pieces)
    channels = pieces[0].shape[1]
    places = [place for _, place in plan]
    base = min(places)
    size = (max(places) - base + 1) * CAP
    return pl.pallas_call(
        functools.partial(away_kernel, sources=sources, plan=plan, base=base),
        in_specs=[IN_HBM] * sources + [IN_VMEM] * 2,
        out_specs=[IN_VMEM] * sources,
        out_shape=[jax.ShapeDtypeStruct((size, channels), BF16)] * sources,
        scratch_shapes=[pltpu.VMEM((sources, size, channels), BF16), pltpu.SemaphoreType.DMA((sources,))],
        compiler_params=pltpu.CompilerParams(vmem_limit_bytes=24 * MIB),
        cost_estimate=pl.CostEstimate(flops=3_000_000_000, bytes_accessed=1 << 20, transcendentals=0),
    )(*[keep_out(p) for p in pieces], *held)


def lat_lon_pairs(lat_step, lon_step):
    bands, sectors = lax.axis_size("lat"), lax.axis_size("lon")
    pairs = []
    for i in range(bands):
        for j in range(sectors):
            target = (i + lat_step) % bands * sectors + (j + lon_step) % sectors
            pairs.append((i * sectors + j, target))
    return pairs


def shift(value, lat_step, lon_step):
    return lax.ppermute(value, ("lat", "lon"), lat_lon_pairs(lat_step, lon_step))


def between(value, distance):
    sectors = lax.axis_size("lon")
    return lax.ppermute(value, "lon", [(s, s ^ distance) for s in range(sectors)])


def per_device(tokens, expert_ids, norm_gain, weight_qkv, weight_proj, temper, router, weight_in, weight_out):
    row_count, col_count, channels = tokens.shape
    token_count = row_count * col_count
    half = token_count // 2
    strip = HALF * HALF
    part = WIN * HALF
    edge = 48
    sectors = lax.axis_size("lon")
    local = weight_in.shape[1]
    pieces_count = sectors // 2
    pair_experts = EXPERTS // pieces_count
    slots = pair_experts * CAP
    lon = lax.axis_index("lon")
    lat = lax.axis_index("lat")

    far_in = between(weight_in, 1)
    far_out = between(weight_out, 1)

    router = router.transpose(0, 2, 1)
    ids = expert_ids.reshape(LAYERS, token_count, 1)
    seam = jnp.where(lat == lax.axis_size("lat") - 1, 1, 0)
    place = jnp.stack([seam, lon // 2, lon % 2]).astype(jnp.int32).reshape(1, 3)

    grid = np.arange(token_count, dtype=np.int32).reshape(row_count // HALF, HALF, col_count // HALF, HALF)
    halves = grid.transpose(0, 2, 1, 3).reshape(2, half)
    order0 = halves.reshape(2, half // part, part).transpose(1, 0, 2).reshape(token_count)
    gap = np.full(strip, -1, np.int32)
    lead = np.full(edge - strip, -1, np.int32)
    low, high = halves
    order1 = np.concatenate([high[strip:], gap, low[strip:], gap, lead, high[:strip], lead, low[:strip]])
    rows1 = order1.shape[0]
    order0, order1 = jnp.asarray(order0), jnp.asarray(order1)

    shape = jax.ShapeDtypeStruct
    piece_shapes = [shape((slots, channels), BF16)] * pieces_count
    attention_scratch = [
        pltpu.VMEM((channels, 3 * channels), BF16), pltpu.VMEM((channels, channels), BF16),
        pltpu.VMEM((token_count, 3 * channels), BF16), pltpu.VMEM((token_count, channels), BF16),
        pltpu.SemaphoreType.DMA((2,)),
    ]

    layer = 0
    mixed, info, *pieces = call(
        functools.partial(first_kernel, layer=layer, pair_experts=pair_experts),
        [(place, SCALARS), (temper, SCALARS), (tokens.reshape(token_count, channels), None),
         (order0[:, None], None), (ids, of_layer(ids, layer)),
         (norm_gain, of_layer(norm_gain, layer)), (weight_qkv, IN_HBM), (weight_proj, IN_HBM),
         (router, of_layer(router, layer))],
        [shape((token_count, channels), BF16), shape((token_count, 2), F32)] + piece_shapes,
        attention_scratch,
        flops=4_000_000_000,
    )
    columns1, row1 = call(
        functools.partial(slots_kernel, pair_experts=pair_experts),
        [(place, SCALARS), (ids, of_layer(ids, 1)), (order1[:, None], None), (info, IN_HBM)],
        [shape((rows1, 2), F32), shape((1, rows1), F32)],
        flops=500_000_000,
    )
    produced = moe(pieces, weight_in, weight_out, far_in, far_out, layer)
    north, own, corner, east = call(
        combine_kernel,
        [(mixed, None), (info, None)] + [(p, None) for p in produced],
        [shape((half, channels), BF16)] * 2 + [shape((edge, channels), BF16)] * 2,
        flops=1_000_000_000,
    )

    layer = 1
    north = shift(north, -1, 0)
    east = shift(east, 0, -1)
    corner = shift(corner, -1, -1)
    low, high, low_edge, high_edge = call(
        functools.partial(shifted_kernel, layer=layer),
        [(place, SCALARS), (temper, SCALARS), (own, None), (north, None), (east, None), (corner, None),
         (norm_gain, of_layer(norm_gain, layer)), (weight_qkv, IN_HBM), (weight_proj, IN_HBM)],
        [shape((half, channels), BF16)] * 2 + [shape((edge, channels), BF16)] * 2,
        [pltpu.VMEM((half + edge, channels), F32)] * 2 + attention_scratch,
        flops=3_000_000_000,
    )
    high = shift(high, 1, 0)
    low_edge = shift(low_edge, 0, 1)
    high_edge = shift(high_edge, 1, 1)
    mixed, info, *pieces = call(
        route_kernel,
        [(low, None), (high, None), (low_edge, None), (high_edge, None), (columns1, None), (row1, None),
         (norm_gain, of_layer(norm_gain, layer)), (router, of_layer(router, layer))],
        [shape((rows1, channels), BF16), shape((rows1, 2), F32)] + piece_shapes,
        flops=1_000_000_000,
    )
    produced = moe(pieces, weight_in, weight_out, far_in, far_out, layer)
    (out,) = call(
        last_kernel,
        [(mixed, None), (info, None), (order1[None, :], None)] + [(p, None) for p in produced],
        [shape((token_count, channels), BF16)],
        flops=1_000_000_000,
    )
    return out.reshape(row_count, col_count, channels)


def moe(pieces, own_in, own_out, far_in, far_out, layer):
    local = own_in.shape[1]
    count = len(pieces)
    if local > 1:
        plan = [(0, entry, entry // 2) for entry in range(local)]
        plan += [(1, entry, local // 2 + entry // 2) for entry in range(local)]
    else:
        plan = [(0, 0, 0), (1, 0, 0)]
    places = sorted({place for _, _, place in plan})
    groups = [places[: len(places) // 2], places[len(places) // 2 :]] if len(places) > 1 else [places]
    near, away = range(count // 2), range(count // 2, count)
    arrived = {k: between(pieces[k], 2 * k) for k in away}
    arrived.update({k: between(pieces[k], 2 * k) if k else pieces[k] for k in near})
    back = {k: [] for k in range(count)}
    outs, held = run_near([arrived[k] for k in near], [own_in, own_out, far_in, far_out], plan, layer)
    for k, value in zip(near, outs):
        back[k].append(between(value, 2 * k) if k else value)
    for group in groups:
        units = [(unit, place) for unit, (_, _, place) in enumerate(plan) if place in group]
        outs = run_away([arrived[k] for k in away], held, units, layer)
        for k, value in zip(away, outs):
            back[k].append(between(value, 2 * k))
    return [value for k in range(count) for value in back[k]]


def solution(mesh):
    in_specs = (
        P("lat", "lon", None),
        P(None, "lat", "lon", None, None),
        P(),
        P(),
        P(),
        P(),
        P(),
        P(None, "lon", None, None),
        P(None, "lon", None, None),
    )
    out_specs = P("lat", "lon", None)
    return jax.shard_map(per_device, mesh=mesh, in_specs=in_specs, out_specs=out_specs, check_vma=False)
```

```python
import functools
import math

import jax
import jax.numpy as jnp
import numpy as np
from jax import lax
from jax.experimental import pallas as pl
from jax.experimental.pallas import tpu as pltpu
from jax.sharding import PartitionSpec as P

WIN = 12
HALF = WIN // 2
EXPERTS = 16
LAYERS = 2
CAP = 48
EPSILON = 1e-05
LANES = 128
MIB = 1 << 20

F32 = jnp.float32
BF16 = jnp.bfloat16


def norm_rows(values, gain_row):
    centered = values - jnp.mean(values, axis=-1, keepdims=True)
    variance = jnp.mean(centered * centered, axis=-1, keepdims=True)
    return (centered * lax.rsqrt(variance + EPSILON) * gain_row).astype(BF16)


def dot(left, right, dims=((1,), (0,))):
    return lax.dot_general(left, right, (dims, ((), ())), preferred_element_type=F32)


def one_hot_columns(column, count):
    spread = lax.broadcasted_iota(jnp.int32, (column.shape[0], count), 1)
    return jnp.where(spread == column, 1.0, 0.0).astype(BF16)


def one_hot_rows(row, count):
    spread = lax.broadcasted_iota(jnp.int32, (count, row.shape[1]), 0)
    return jnp.where(spread == row, 1.0, 0.0).astype(BF16)


class Brought:
    def __init__(self, source, target, arrived):
        self.target, self.pending = target, True
        self.copy = pltpu.make_async_copy(source, target, arrived)
        self.copy.start()

    def get(self):
        if self.pending:
            self.copy.wait()
            self.pending = False
        return self.target[...]


def upright(row):
    return jnp.transpose(jnp.broadcast_to(row.astype(F32), (LANES, row.shape[1])))


def slots_of(ids_row, order, place_ref, pair_experts):
    count = ids_row.shape[1]
    spread_ids = upright(ids_row).astype(jnp.int32)
    ids = spread_ids[:, 0:1]
    chosen = lax.broadcasted_iota(jnp.int32, (count, LANES), 1) == spread_ids
    earlier = lax.broadcasted_iota(jnp.int32, (count, count), 0) > lax.broadcasted_iota(jnp.int32, (count, count), 1)
    before = dot(jnp.where(earlier, 1.0, 0.0).astype(BF16), jnp.where(chosen, 1.0, 0.0).astype(BF16))
    place = jnp.sum(jnp.where(chosen, before, 0.0), axis=1, keepdims=True).astype(jnp.int32)
    piece = lax.div(ids, pair_experts) ^ place_ref[0, 1]
    inner = lax.rem(ids, pair_experts) ^ (place_ref[0, 2] * (pair_experts // 2))
    target = (piece * pair_experts + inner) * CAP + place
    lane = lax.broadcasted_iota(jnp.int32, (count, LANES), 1)
    parts = jnp.where(lane == 0, target // 256, jnp.where(lane == 1, target % 256, jnp.where(lane == 2, ids, 1)))
    moved = dot(one_hot_columns(order, count), parts.astype(F32).astype(BF16))
    slot = jnp.where(moved[:, 3:4] > 0.5, moved[:, 0:1] * 256.0 + moved[:, 1:2], -1.0)
    row = jnp.transpose(jnp.broadcast_to(slot, (slot.shape[0], LANES)))[0:1, :]
    return moved[:, 2:3], slot, row


def route(ynorm, router, experts, target_row, piece_refs):
    logits = dot(ynorm, router, ((1,), (1,)))
    chosen = lax.broadcasted_iota(jnp.int32, logits.shape, 1) == experts.astype(jnp.int32)
    picked = jnp.sum(jnp.where(chosen, logits, 0.0), axis=1, keepdims=True)
    target = target_row.astype(jnp.int32)
    slots = piece_refs[0].shape[0]
    for index, piece_ref in enumerate(piece_refs):
        spread = one_hot_rows(target - index * slots, slots)
        piece_ref[...] = dot(spread, ynorm).astype(BF16)
    return jax.nn.sigmoid(picked)


def attend(frame, layer, place_ref, temper_ref, gain, wqkv, wproj, qkv_ref, context_ref):
    total, channels = frame.shape
    heads = temper_ref.shape[1]
    width = channels // heads
    area = WIN * WIN
    windows = total // area
    group = LANES // width
    main = LANES
    rest = area - main
    lanes = group * area
    normed = norm_rows(frame, gain.get()[0:1, :])
    qkv_ref[...] = dot(normed, wqkv.get()).astype(BF16)

    lane = lax.broadcasted_iota(jnp.int32, (1, lanes), 1)
    leftover = lane >= group * main
    head_of = jnp.where(leftover, (lane - group * main) // rest, lane // main)
    query_of = jnp.where(leftover, main + (lane - group * main) % rest, lane % main)
    late = query_of >= area // 2
    seam = place_ref[0, 0] > 0
    bias_early = jnp.where(jnp.logical_and(seam, late), -1e30, 0.0)
    bias_late = jnp.where(jnp.logical_and(seam, jnp.logical_not(late)), -1e30, 0.0)
    channel_head = lax.broadcasted_iota(jnp.int32, (1, LANES), 1) // width
    keep = [jnp.where(channel_head == h, 1.0, 0.0).astype(BF16) for h in range(group)]
    keep_f = [jnp.where(channel_head == h, 1.0, 0.0) for h in range(group)]

    def one_window(window):
        rows = pl.ds(window * area, area)
        for g in range(channels // LANES):
            q = qkv_ref[rows, g * LANES : (g + 1) * LANES]
            k = qkv_ref[rows, channels + g * LANES : channels + (g + 1) * LANES]
            v = qkv_ref[rows, 2 * channels + g * LANES : 2 * channels + (g + 1) * LANES]
            stacked = jnp.concatenate(
                [q[:main] * keep[h] for h in range(group)] + [q[main:] * keep[h] for h in range(group)], axis=0
            )
            scores = dot(k, stacked, ((1,), (1,)))
            scale = jnp.zeros((1, lanes), F32)
            for h in range(group):
                factor = temper_ref[layer, g * group + h] * (math.log2(math.e) / math.sqrt(width))
                scale = jnp.where(head_of == h, factor, scale)
            if layer % 2 == 1:
                scores = jnp.concatenate(
                    [scores[: area // 2] + bias_early, scores[area // 2 :] + bias_late], axis=0
                )
            peak = jnp.max(scores, axis=0, keepdims=True)
            weights = jnp.exp2((scores - peak) * scale)
            shares = (weights * (1.0 / jnp.sum(weights, axis=0, keepdims=True))).astype(BF16)
            mixed_t = dot(v, shares, ((0,), (0,)))
            picked = jnp.concatenate(
                [mixed_t[h * width : (h + 1) * width, h * main : (h + 1) * main] for h in range(group)], axis=0
            )
            first = jnp.transpose(picked)
            tail = jnp.transpose(mixed_t[:, group * main :])
            second = tail[:rest] * keep_f[0]
            for h in range(1, group):
                second = second + tail[h * rest : (h + 1) * rest] * keep_f[h]
            context = jnp.concatenate([first, second], axis=0).astype(BF16)
            context_ref[rows, g * LANES : (g + 1) * LANES] = context

    for window in range(windows):
        one_window(window)
    attended = dot(context_ref[...], wproj.get())
    return (frame + attended).astype(BF16)


def first_kernel(
    place_ref, temper_ref, tokens, order, ids, gain, wqkv, wproj, router,
    mixed_ref, info_ref, *refs, layer, pair_experts
):
    *piece_refs, qkv_ref, context_ref = refs
    order = upright(order.get())[:, 0:1].astype(jnp.int32)
    rows = tokens.get()
    frame = dot(one_hot_columns(order, rows.shape[0]), rows)
    mixed = attend(frame, layer, place_ref, temper_ref, gain, wqkv, wproj, qkv_ref, context_ref)
    mixed_ref[...] = mixed
    ynorm = norm_rows(mixed.astype(F32), gain.get()[1:2, :])
    experts, slot, slot_row = slots_of(ids.get(), order, place_ref, pair_experts)
    gate = route(ynorm, router.get(), experts, slot_row, piece_refs)
    info_ref[...] = jnp.concatenate([gate, slot], axis=1)


def slots_kernel(place_ref, ids, order, _, columns_ref, row_ref, *, pair_experts):
    order = upright(order.get())[:, 0:1].astype(jnp.int32)
    experts, slot, slot_row = slots_of(ids.get(), order, place_ref, pair_experts)
    columns_ref[...] = jnp.concatenate([experts, slot], axis=1)
    row_ref[...] = slot_row


def shifted_kernel(
    place_ref, temper_ref, own_ref, north_ref, east_ref, corner_ref, gain, wqkv, wproj,
    low_ref, high_ref, low_edge_ref, high_edge_ref,
    low_scratch, high_scratch, qkv_ref, context_ref, *, layer
):
    half, channels = own_ref.shape
    strip = HALF * HALF
    part = WIN * HALF
    edge = east_ref.shape[0]
    low_scratch[0:half] = own_ref[...].astype(F32)
    low_scratch[half : half + edge] = east_ref[...].astype(F32)
    high_scratch[0:half] = north_ref[...].astype(F32)
    high_scratch[half : half + edge] = corner_ref[...].astype(F32)
    pieces = []
    for window in range(half // part):
        start = strip + window * part
        pieces += [low_scratch[start : start + part], high_scratch[start : start + part]]
    frame = jnp.concatenate(pieces, axis=0)
    mixed = attend(frame, layer, place_ref, temper_ref, gain, wqkv, wproj, qkv_ref, context_ref)
    mixed = mixed.astype(F32)
    low, high = split_halves(mixed)
    low_ref[...] = low.astype(BF16)
    high_ref[...] = high.astype(BF16)
    low_edge_ref[...] = low[half - edge :].astype(BF16)
    high_edge_ref[...] = high[half - edge :].astype(BF16)


def split_halves(rows):
    part = WIN * HALF
    pieces = [rows[start : start + part] for start in range(0, rows.shape[0], part)]
    return jnp.concatenate(pieces[0::2], axis=0), jnp.concatenate(pieces[1::2], axis=0)


def route_kernel(own_ref, south_ref, west_ref, corner_ref, columns_ref, row_ref, gain, router,
                 rows_ref, info_ref, *piece_refs):
    mixed = jnp.concatenate([own_ref[...], south_ref[...], west_ref[...], corner_ref[...]], axis=0)
    rows_ref[...] = mixed
    ynorm = norm_rows(mixed.astype(F32), gain.get()[1:2, :])
    gate = route(ynorm, router.get(), columns_ref[:, 0:1], row_ref[...], piece_refs)
    info_ref[...] = jnp.concatenate([gate, columns_ref[:, 1:2]], axis=1)


def expert_rows(piece_refs, out_refs, block, first, second, carried, last):
    rows = jnp.concatenate([ref[block, :] for ref in piece_refs], axis=0)
    hidden = jax.nn.gelu(dot(rows, first())).astype(BF16)
    part = dot(hidden, second())
    total = part if carried is None else carried + part
    if last:
        for index, ref in enumerate(out_refs):
            ref[block, :] = total[index * CAP : (index + 1) * CAP].astype(BF16)
    return total


def near_kernel(*refs, plan, layer):
    piece_ref, *weights = refs[:5]
    out_ref, first_ref, second_ref, arrived = refs[5:]
    ahead = 2
    copies = {}

    def begin(unit):
        if unit < len(plan):
            which, entry, _ = plan[unit]
            for side, target in enumerate((first_ref, second_ref)):
                copies[unit, side] = pltpu.make_async_copy(
                    weights[2 * which + side].at[layer, entry], target.at[unit], arrived.at[side, unit]
                )
                copies[unit, side].start()

    def wait_for(unit, side, ref):
        copies[unit, side].wait()
        if side == 0:
            begin(unit + ahead)
        return ref[unit]

    for unit in range(ahead):
        begin(unit)
    totals = {}
    last = {place: unit for unit, (_, _, place) in enumerate(plan)}
    for unit, (_, _, place) in enumerate(plan):
        block = slice(place * CAP, (place + 1) * CAP)
        totals[place] = expert_rows(
            [piece_ref], [out_ref], block,
            functools.partial(wait_for, unit, 0, first_ref), functools.partial(wait_for, unit, 1, second_ref),
            totals.get(place), last[place] == unit,
        )


def away_kernel(*refs, sources, plan, base, kept):
    piece_refs = refs[:sources]
    first_ref, second_ref = refs[sources : sources + 2]
    kept_refs = refs[sources + 2 : sources + 2 + kept]
    out_refs = list(refs[sources + 2 + kept :])
    for index, ref in enumerate(kept_refs):
        size = ref.shape[0]
        out_refs[index][0:size, :] = ref[...]
        out_refs[index] = out_refs[index].at[size:]
    totals = {}
    last = {place: unit for unit, place in plan}
    for unit, place in plan:
        outs = [ref.at[pl.ds((place - base) * CAP, CAP)] for ref in out_refs]
        block = slice(place * CAP, (place + 1) * CAP)
        rows = jnp.concatenate([ref[block, :] for ref in piece_refs], axis=0)
        hidden = jax.nn.gelu(dot(rows, first_ref[unit])).astype(BF16)
        part = dot(hidden, second_ref[unit])
        totals[place] = totals[place] + part if place in totals else part
        if last[place] == unit:
            for index, ref in enumerate(outs):
                ref[...] = totals[place][index * CAP : (index + 1) * CAP].astype(BF16)


def gathered_state(mixed_ref, info_ref, piece_refs):
    produced = jnp.concatenate([ref[...] for ref in piece_refs], axis=0)
    spread = one_hot_columns(info_ref[:, 1:2].astype(jnp.int32), produced.shape[0])
    combined = dot(spread, produced)
    return (mixed_ref[...].astype(F32) + info_ref[:, 0:1] * combined).astype(BF16)


def combine_kernel(mixed_ref, info_ref, *refs):
    *piece_refs, north_ref, own_ref, corner_ref, east_ref = refs
    state = gathered_state(mixed_ref, info_ref, piece_refs).astype(F32)
    low, high = split_halves(state)
    edge = east_ref.shape[0]
    north_ref[...] = low.astype(BF16)
    own_ref[...] = high.astype(BF16)
    corner_ref[...] = low[:edge].astype(BF16)
    east_ref[...] = high[:edge].astype(BF16)


def last_kernel(mixed_ref, info_ref, order, *refs):
    *piece_refs, out_ref = refs
    state = gathered_state(mixed_ref, info_ref, piece_refs)
    out_ref[...] = dot(one_hot_rows(order.get(), out_ref.shape[0]), state).astype(BF16)


SCALARS = pl.BlockSpec(memory_space=pltpu.SMEM)
IN_HBM = pl.BlockSpec(memory_space=pltpu.HBM)
IN_VMEM = pl.BlockSpec(memory_space=pltpu.VMEM)
UNREAD = "unread"


def keep_out(array):
    return pltpu.with_memory_space_constraint(array, pltpu.HBM)


def call(kernel, ins, outs, scratch=(), limit=40, flops=0):
    arrays, specs, rooms = [], [], []
    for array, how in ins:
        specs.append(how if how in (SCALARS, IN_VMEM) else IN_HBM)
        arrays.append(array if how == IN_VMEM else keep_out(array))
        if isinstance(how, tuple):
            rooms.append(pltpu.VMEM(array.shape[len(how) :], array.dtype))
    brought = len(rooms)

    def body(*refs):
        operands = list(refs[: len(ins)])
        room_refs, arrived = (refs[-1 - brought : -1], refs[-1]) if brought else ((), None)
        others = refs[len(ins) : len(refs) - (brought + 1 if brought else 0)]
        at = 0
        for index, (_, how) in enumerate(ins):
            if isinstance(how, tuple):
                source = operands[index].at[how] if how else operands[index]
                operands[index] = Brought(source, room_refs[at], arrived.at[at])
                at += 1
        kernel(*operands, *others)

    size = sum(a.size * a.dtype.itemsize for a in arrays)
    return pl.pallas_call(
        body,
        in_specs=specs,
        out_specs=[IN_VMEM] * len(outs),
        out_shape=outs,
        scratch_shapes=list(scratch) + rooms + ([pltpu.SemaphoreType.DMA((brought,))] if brought else []),
        compiler_params=pltpu.CompilerParams(vmem_limit_bytes=limit * MIB),
        cost_estimate=pl.CostEstimate(flops=flops, bytes_accessed=size, transcendentals=0),
    )(*arrays)


def run_near(piece, weights, plan, layer):
    channels, units = piece.shape[1], weights[0].shape[3]
    held = [pltpu.VMEM((len(plan), channels, units), BF16), pltpu.VMEM((len(plan), units, channels), BF16)]
    out, *held = pl.pallas_call(
        functools.partial(near_kernel, plan=plan, layer=layer),
        in_specs=[IN_VMEM] + [IN_HBM] * 4,
        out_specs=[IN_VMEM] * 3,
        out_shape=[jax.ShapeDtypeStruct(piece.shape, BF16)] + held,
        scratch_shapes=[pltpu.SemaphoreType.DMA((2, len(plan)))],
        compiler_params=pltpu.CompilerParams(vmem_limit_bytes=24 * MIB),
        cost_estimate=pl.CostEstimate(
            flops=4_000_000_000, bytes_accessed=len(plan) * 4 * channels * units, transcendentals=0
        ),
    )(piece, *[keep_out(w) for w in weights])
    return out, held


def run_away(pieces, held, plan, kept):
    sources = len(pieces)
    channels = pieces[0].shape[1]
    places = [place for _, place in plan]
    base = min(places)
    size = (max(places) - base + 1) * CAP
    sizes = [size + kept[k].shape[0] if k < len(kept) else size for k in range(sources)]
    return pl.pallas_call(
        functools.partial(away_kernel, sources=sources, plan=plan, base=base, kept=len(kept)),
        in_specs=[IN_VMEM] * (sources + 2 + len(kept)),
        out_specs=[IN_VMEM] * sources,
        out_shape=[jax.ShapeDtypeStruct((rows, channels), BF16) for rows in sizes],
        compiler_params=pltpu.CompilerParams(vmem_limit_bytes=24 * MIB),
        cost_estimate=pl.CostEstimate(flops=3_000_000_000, bytes_accessed=1 << 20, transcendentals=0),
    )(*pieces, *held, *kept)


def lat_lon_pairs(lat_step, lon_step):
    bands, sectors = lax.axis_size("lat"), lax.axis_size("lon")
    pairs = []
    for i in range(bands):
        for j in range(sectors):
            target = (i + lat_step) % bands * sectors + (j + lon_step) % sectors
            pairs.append((i * sectors + j, target))
    return pairs


def shift(value, lat_step, lon_step):
    return lax.ppermute(value, ("lat", "lon"), lat_lon_pairs(lat_step, lon_step))


def between(value, distance):
    sectors = lax.axis_size("lon")
    return lax.ppermute(value, "lon", [(s, s ^ distance) for s in range(sectors)])


def per_device(tokens, expert_ids, norm_gain, weight_qkv, weight_proj, temper, router, weight_in, weight_out):
    row_count, col_count, channels = tokens.shape
    token_count = row_count * col_count
    half = token_count // 2
    strip = HALF * HALF
    part = WIN * HALF
    edge = 48
    sectors = lax.axis_size("lon")
    local = weight_in.shape[1]
    pieces_count = sectors // 2
    pair_experts = EXPERTS // pieces_count
    slots = pair_experts * CAP
    lon = lax.axis_index("lon")
    lat = lax.axis_index("lat")

    far_in = between(weight_in, 1)
    far_out = between(weight_out, 1)

    router = router.transpose(0, 2, 1)
    ids = expert_ids.reshape(LAYERS, 1, token_count)
    seam = jnp.where(lat == lax.axis_size("lat") - 1, 1, 0)
    place = jnp.stack([seam, lon // 2, lon % 2]).astype(jnp.int32).reshape(1, 3)

    grid = np.arange(token_count, dtype=np.int32).reshape(row_count // HALF, HALF, col_count // HALF, HALF)
    halves = grid.transpose(0, 2, 1, 3).reshape(2, half)
    order0 = halves.reshape(2, half // part, part).transpose(1, 0, 2).reshape(token_count)
    gap = np.full(strip, -1, np.int32)
    lead = np.full(edge - strip, -1, np.int32)
    low, high = halves
    order1 = np.concatenate([high[strip:], gap, low[strip:], gap, lead, high[:strip], lead, low[:strip]])
    rows1 = order1.shape[0]
    order0, order1 = jnp.asarray(order0)[None], jnp.asarray(order1)[None]

    shape = jax.ShapeDtypeStruct
    piece_shapes = [shape((slots, channels), BF16)] * pieces_count
    attention_scratch = [
        pltpu.VMEM((token_count, 3 * channels), BF16), pltpu.VMEM((token_count, channels), BF16),
    ]

    layer = 0
    mixed, info, *pieces = call(
        functools.partial(first_kernel, layer=layer, pair_experts=pair_experts),
        [(place, SCALARS), (temper, SCALARS), (tokens.reshape(token_count, channels), ()),
         (order0, ()), (ids, (layer,)),
         (norm_gain, (layer,)), (weight_qkv, (layer,)), (weight_proj, (layer,)), (router, (layer,))],
        [shape((token_count, channels), BF16), shape((token_count, 2), F32)] + piece_shapes,
        attention_scratch,
        flops=4_000_000_000,
    )
    columns1, row1 = call(
        functools.partial(slots_kernel, pair_experts=pair_experts),
        [(place, SCALARS), (ids, (1,)), (order1, ()), (info, IN_VMEM)],
        [shape((rows1, 2), F32), shape((1, rows1), F32)],
        flops=500_000_000,
    )
    produced = moe(pieces, weight_in, weight_out, far_in, far_out, layer)
    north, own, corner, east = call(
        combine_kernel,
        [(mixed, IN_VMEM), (info, IN_VMEM)] + [(p, IN_VMEM) for p in produced],
        [shape((half, channels), BF16)] * 2 + [shape((edge, channels), BF16)] * 2,
        flops=1_000_000_000,
    )

    layer = 1
    north = shift(north, -1, 0)
    east = shift(east, 0, -1)
    corner = shift(corner, -1, -1)
    low, high, low_edge, high_edge = call(
        functools.partial(shifted_kernel, layer=layer),
        [(place, SCALARS), (temper, SCALARS), (own, IN_VMEM), (north, IN_VMEM), (east, IN_VMEM), (corner, IN_VMEM),
         (norm_gain, (layer,)), (weight_qkv, (layer,)), (weight_proj, (layer,))],
        [shape((half, channels), BF16)] * 2 + [shape((edge, channels), BF16)] * 2,
        [pltpu.VMEM((half + edge, channels), F32)] * 2 + attention_scratch,
        flops=3_000_000_000,
    )
    high = shift(high, 1, 0)
    low_edge = shift(low_edge, 0, 1)
    high_edge = shift(high_edge, 1, 1)
    mixed, info, *pieces = call(
        route_kernel,
        [(low, IN_VMEM), (high, IN_VMEM), (low_edge, IN_VMEM), (high_edge, IN_VMEM), (columns1, IN_VMEM),
         (row1, IN_VMEM), (norm_gain, (layer,)), (router, (layer,))],
        [shape((rows1, channels), BF16), shape((rows1, 2), F32)] + piece_shapes,
        flops=1_000_000_000,
    )
    produced = moe(pieces, weight_in, weight_out, far_in, far_out, layer)
    (out,) = call(
        last_kernel,
        [(mixed, IN_VMEM), (info, IN_VMEM), (order1, ())] + [(p, IN_VMEM) for p in produced],
        [shape((token_count, channels), BF16)],
        flops=1_000_000_000,
    )
    return out.reshape(row_count, col_count, channels)


def moe(pieces, own_in, own_out, far_in, far_out, layer):
    local = own_in.shape[1]
    count = len(pieces)
    if local > 1:
        plan = [(0, entry, entry // 2) for entry in range(local)]
        plan += [(1, entry, local // 2 + entry // 2) for entry in range(local)]
    else:
        plan = [(0, 0, 0), (1, 0, 0)]
    places = sorted({place for _, _, place in plan})
    groups = [places[: len(places) // 2], places[len(places) // 2 :]] if len(places) > 1 else [places]
    away = list(range(count // 2, count))
    beside = list(range(1, count // 2))
    arrived = {k: between(pieces[k], 2 * k) for k in away + beside}
    own, held = run_near(pieces[0], [own_in, own_out, far_in, far_out], plan, layer)
    back = {k: [] for k in range(count)}
    kept = []
    for turn, group in enumerate(groups):
        units = [(unit, place) for unit, (_, _, place) in enumerate(plan) if place in group]
        outs = run_away([arrived[k] for k in beside + away], held, units, kept)
        kept = outs[: len(beside)]
        for k, value in zip(away, outs[len(beside) :]):
            back[k].append(between(value, 2 * k))
    back[0] = [own]
    for k, value in zip(beside, kept):
        back[k] = [between(value, 2 * k)]
    return [value for k in range(count) for value in back[k]]


def solution(mesh):
    in_specs = (
        P("lat", "lon", None),
        P(None, "lat", "lon", None, None),
        P(),
        P(),
        P(),
        P(),
        P(),
        P(None, "lon", None, None),
        P(None, "lon", None, None),
    )
    out_specs = P("lat", "lon", None)
    return jax.shard_map(per_device, mesh=mesh, in_specs=in_specs, out_specs=out_specs, check_vma=False)
```

```python
import functools
import math

import jax
import jax.numpy as jnp
import numpy as np
from jax import lax
from jax.experimental import pallas as pl
from jax.experimental.pallas import tpu as pltpu
from jax.sharding import PartitionSpec as P

WIN = 12
HALF = WIN // 2
EXPERTS = 16
LAYERS = 2
CAP = 48
EPSILON = 1e-05
LANES = 128
MIB = 1 << 20

F32 = jnp.float32
BF16 = jnp.bfloat16


def norm_rows(values, gain_row):
    centered = values - jnp.mean(values, axis=-1, keepdims=True)
    variance = jnp.mean(centered * centered, axis=-1, keepdims=True)
    return (centered * lax.rsqrt(variance + EPSILON) * gain_row).astype(BF16)


def dot(left, right, dims=((1,), (0,))):
    return lax.dot_general(left, right, (dims, ((), ())), preferred_element_type=F32)


def one_hot_columns(column, count):
    spread = lax.broadcasted_iota(jnp.int32, (column.shape[0], count), 1)
    return jnp.where(spread == column, 1.0, 0.0).astype(BF16)


def one_hot_rows(row, count):
    spread = lax.broadcasted_iota(jnp.int32, (count, row.shape[1]), 0)
    return jnp.where(spread == row, 1.0, 0.0).astype(BF16)


class Brought:
    def __init__(self, source, target, arrived):
        self.target, self.pending = target, True
        self.copy = pltpu.make_async_copy(source, target, arrived)
        self.copy.start()

    def get(self):
        if self.pending:
            self.copy.wait()
            self.pending = False
        return self.target[...]


def upright(row):
    return jnp.transpose(jnp.broadcast_to(row.astype(F32), (LANES, row.shape[1])))


def slots_of(ids_row, reorder, place_ref, pair_experts):
    count = ids_row.shape[1]
    spread_ids = upright(ids_row).astype(jnp.int32)
    ids = spread_ids[:, 0:1]
    chosen = lax.broadcasted_iota(jnp.int32, (count, LANES), 1) == spread_ids
    earlier = lax.broadcasted_iota(jnp.int32, (count, count), 0) > lax.broadcasted_iota(jnp.int32, (count, count), 1)
    before = dot(jnp.where(earlier, 1.0, 0.0).astype(BF16), jnp.where(chosen, 1.0, 0.0).astype(BF16))
    place = jnp.sum(jnp.where(chosen, before, 0.0), axis=1, keepdims=True).astype(jnp.int32)
    shift_by = pair_experts.bit_length() - 1
    piece = (ids >> shift_by) ^ place_ref[0, 1]
    inner = (ids & (pair_experts - 1)) ^ (place_ref[0, 2] * (pair_experts // 2))
    target = (piece * pair_experts + inner) * CAP + place
    lane = lax.broadcasted_iota(jnp.int32, (count, LANES), 1)
    parts = jnp.where(lane == 0, target >> 8, jnp.where(lane == 1, target & 255, jnp.where(lane == 2, ids, 1)))
    moved = dot(reorder, parts.astype(F32).astype(BF16))
    slot = jnp.where(moved[:, 3:4] > 0.5, moved[:, 0:1] * 256.0 + moved[:, 1:2], -1.0)
    row = jnp.transpose(jnp.broadcast_to(slot, (slot.shape[0], LANES)))[0:1, :]
    return moved[:, 2:3], slot, row


def route(ynorm, router, experts, target_row, piece_refs):
    logits = dot(ynorm, router, ((1,), (1,)))
    chosen = lax.broadcasted_iota(jnp.int32, logits.shape, 1) == experts.astype(jnp.int32)
    picked = jnp.sum(jnp.where(chosen, logits, 0.0), axis=1, keepdims=True)
    target = target_row.astype(jnp.int32)
    start = 0
    for piece_ref in piece_refs:
        slots = piece_ref.shape[0]
        piece_ref[...] = dot(one_hot_rows(target - start, slots), ynorm).astype(BF16)
        start += slots
    return jax.nn.sigmoid(picked)


def attend(frame, layer, place_ref, temper_ref, gain, wqkv, wproj, qkv_ref, context_ref):
    total, channels = frame.shape
    heads = temper_ref.shape[1]
    width = channels // heads
    area = WIN * WIN
    windows = total // area
    group = LANES // width
    main = LANES
    rest = area - main
    lanes = group * area
    normed = norm_rows(frame, gain.get()[0:1, :])
    qkv_ref[...] = dot(normed, wqkv()).astype(BF16)

    lane = lax.broadcasted_iota(jnp.int32, (1, lanes), 1)
    leftover = lane >= group * main
    head_of = jnp.where(leftover, (lane - group * main) // rest, lane // main)
    query_of = jnp.where(leftover, main + (lane - group * main) % rest, lane % main)
    late = query_of >= area // 2
    seam = place_ref[0, 0] > 0
    bias_early = jnp.where(jnp.logical_and(seam, late), -1e30, 0.0)
    bias_late = jnp.where(jnp.logical_and(seam, jnp.logical_not(late)), -1e30, 0.0)
    channel_head = lax.broadcasted_iota(jnp.int32, (1, LANES), 1) // width
    keep = [jnp.where(channel_head == h, 1.0, 0.0).astype(BF16) for h in range(group)]
    keep_f = [jnp.where(channel_head == h, 1.0, 0.0) for h in range(group)]

    def one_window(window):
        rows = pl.ds(window * area, area)
        for g in range(channels // LANES):
            q = qkv_ref[rows, g * LANES : (g + 1) * LANES]
            k = qkv_ref[rows, channels + g * LANES : channels + (g + 1) * LANES]
            v = qkv_ref[rows, 2 * channels + g * LANES : 2 * channels + (g + 1) * LANES]
            stacked = jnp.concatenate(
                [q[:main] * keep[h] for h in range(group)] + [q[main:] * keep[h] for h in range(group)], axis=0
            )
            scores = dot(k, stacked, ((1,), (1,)))
            scale = jnp.zeros((1, lanes), F32)
            for h in range(group):
                factor = temper_ref[layer, g * group + h] * (math.log2(math.e) / math.sqrt(width))
                scale = jnp.where(head_of == h, factor, scale)
            if layer % 2 == 1:
                scores = jnp.concatenate(
                    [scores[: area // 2] + bias_early, scores[area // 2 :] + bias_late], axis=0
                )
            peak = jnp.max(scores, axis=0, keepdims=True)
            weights = jnp.exp2((scores - peak) * scale)
            shares = (weights * (1.0 / jnp.sum(weights, axis=0, keepdims=True))).astype(BF16)
            mixed_t = dot(v, shares, ((0,), (0,)))
            picked = jnp.concatenate(
                [mixed_t[h * width : (h + 1) * width, h * main : (h + 1) * main] for h in range(group)], axis=0
            )
            first = jnp.transpose(picked)
            tail = jnp.transpose(mixed_t[:, group * main :])
            second = tail[:rest] * keep_f[0]
            for h in range(1, group):
                second = second + tail[h * rest : (h + 1) * rest] * keep_f[h]
            context = jnp.concatenate([first, second], axis=0).astype(BF16)
            context_ref[rows, g * LANES : (g + 1) * LANES] = context

    for window in range(windows):
        one_window(window)
    attended = dot(context_ref[...], wproj())
    return (frame + attended).astype(BF16)


def first_kernel(
    place_ref, temper_ref, tokens, order, ids, gain, wqkv, wproj, router,
    mixed_ref, info_ref, *refs, layer, pair_experts
):
    *piece_refs, qkv_ref, context_ref = refs
    reorder = one_hot_columns(upright(order.get())[:, 0:1].astype(jnp.int32), order.target.shape[1])
    experts, slot, slot_row = slots_of(ids.get(), reorder, place_ref, pair_experts)
    frame = dot(reorder, tokens.get())
    mixed = attend(frame, layer, place_ref, temper_ref, gain, wqkv.get, wproj.get, qkv_ref, context_ref)
    mixed_ref[...] = mixed
    ynorm = norm_rows(mixed.astype(F32), gain.get()[1:2, :])
    gate = route(ynorm, router.get(), experts, slot_row, piece_refs)
    info_ref[...] = jnp.concatenate([gate, slot], axis=1)


def ahead_kernel(place_ref, ids, order, wqkv_hbm, wproj_hbm, _, columns_ref, row_ref, wqkv_ref, wproj_ref, arrived,
                 *, layer, pair_experts):
    copies = [
        pltpu.make_async_copy(source.at[layer], target, arrived.at[index])
        for index, (source, target) in enumerate(((wqkv_hbm, wqkv_ref), (wproj_hbm, wproj_ref)))
    ]
    for copy in copies:
        copy.start()
    ids_row = ids.get()
    reorder = one_hot_columns(upright(order.get())[:, 0:1].astype(jnp.int32), ids_row.shape[1])
    experts, slot, slot_row = slots_of(ids_row, reorder, place_ref, pair_experts)
    columns_ref[...] = jnp.concatenate([experts, slot], axis=1)
    row_ref[...] = slot_row
    for copy in copies:
        copy.wait()


def shifted_kernel(
    place_ref, temper_ref, own_ref, north_ref, east_ref, corner_ref, gain, wqkv_ref, wproj_ref,
    low_ref, high_ref, low_edge_ref, high_edge_ref,
    low_scratch, high_scratch, qkv_ref, context_ref, *, layer
):
    half, channels = own_ref.shape
    strip = HALF * HALF
    part = WIN * HALF
    edge = east_ref.shape[0]
    low_scratch[0:half] = own_ref[...].astype(F32)
    low_scratch[half : half + edge] = east_ref[...].astype(F32)
    high_scratch[0:half] = north_ref[...].astype(F32)
    high_scratch[half : half + edge] = corner_ref[...].astype(F32)
    pieces = []
    for window in range(half // part):
        start = strip + window * part
        pieces += [low_scratch[start : start + part], high_scratch[start : start + part]]
    frame = jnp.concatenate(pieces, axis=0)
    mixed = attend(
        frame, layer, place_ref, temper_ref, gain, lambda: wqkv_ref[...], lambda: wproj_ref[...], qkv_ref, context_ref
    )
    mixed = mixed.astype(F32)
    low, high = split_halves(mixed)
    low_ref[...] = low.astype(BF16)
    high_ref[...] = high.astype(BF16)
    low_edge_ref[...] = low[half - edge :].astype(BF16)
    high_edge_ref[...] = high[half - edge :].astype(BF16)


def split_halves(rows):
    part = WIN * HALF
    pieces = [rows[start : start + part] for start in range(0, rows.shape[0], part)]
    return jnp.concatenate(pieces[0::2], axis=0), jnp.concatenate(pieces[1::2], axis=0)


def route_kernel(own_ref, south_ref, west_ref, corner_ref, columns_ref, row_ref, gain, router,
                 rows_ref, info_ref, *piece_refs):
    mixed = jnp.concatenate([own_ref[...], south_ref[...], west_ref[...], corner_ref[...]], axis=0)
    rows_ref[...] = mixed
    ynorm = norm_rows(mixed.astype(F32), gain.get()[1:2, :])
    gate = route(ynorm, router.get(), columns_ref[:, 0:1], row_ref[...], piece_refs)
    info_ref[...] = jnp.concatenate([gate, columns_ref[:, 1:2]], axis=1)


def expert_rows(piece_refs, starts, out_refs, first, second, carried, last):
    rows = jnp.concatenate([ref[start : start + CAP, :] for ref, start in zip(piece_refs, starts)], axis=0)
    hidden = jax.nn.gelu(dot(rows, first())).astype(BF16)
    part = dot(hidden, second())
    total = part if carried is None else carried + part
    if last:
        for index, (ref, start) in enumerate(out_refs):
            ref[start : start + CAP, :] = total[index * CAP : (index + 1) * CAP].astype(BF16)
    return total


def near_kernel(*refs, plan, base, layer):
    piece_ref = refs[0]
    weights = refs[1:-4]
    out_ref, first_ref, second_ref, arrived = refs[-4:]
    ahead = 2
    copies = {}

    def begin(unit):
        if unit < len(plan):
            which, entry, _ = plan[unit]
            for side, target in enumerate((first_ref, second_ref)):
                copies[unit, side] = pltpu.make_async_copy(
                    weights[2 * which + side].at[layer, entry], target.at[unit], arrived.at[side, unit]
                )
                copies[unit, side].start()

    def wait_for(unit, side, ref):
        copies[unit, side].wait()
        if side == 0:
            begin(unit + ahead)
        return ref[unit]

    for unit in range(ahead):
        begin(unit)
    totals = {}
    last = {place: unit for unit, (_, _, place) in enumerate(plan)}
    for unit, (_, _, place) in enumerate(plan):
        start = (place - base) * CAP
        totals[place] = expert_rows(
            [piece_ref], [start], [(out_ref, start)],
            functools.partial(wait_for, unit, 0, first_ref), functools.partial(wait_for, unit, 1, second_ref),
            totals.get(place), last[place] == unit,
        )


def away_kernel(*refs, whole, cut, plan, base, kept):
    piece_refs = refs[: whole + cut]
    first_ref, second_ref = refs[whole + cut : whole + cut + 2]
    kept_refs = refs[whole + cut + 2 : whole + cut + 2 + kept]
    out_refs = refs[whole + cut + 2 + kept :]
    lead = [0] * (whole + cut)
    for index, ref in enumerate(kept_refs):
        lead[index] = ref.shape[0]
        out_refs[index][0 : lead[index], :] = ref[...]
    totals = {}
    last = {place: unit for unit, (_, _, place) in enumerate(plan)}
    for unit, (_, _, place) in enumerate(plan):
        inner = (place - base) * CAP
        totals[place] = expert_rows(
            piece_refs, [place * CAP] * whole + [inner] * cut,
            [(ref, start + inner) for ref, start in zip(out_refs, lead)],
            lambda unit=unit: first_ref[unit], lambda unit=unit: second_ref[unit],
            totals.get(place), last[place] == unit,
        )


def gathered_state(mixed_ref, info_ref, piece_refs):
    produced = jnp.concatenate([ref[...] for ref in piece_refs], axis=0)
    spread = one_hot_columns(info_ref[:, 1:2].astype(jnp.int32), produced.shape[0])
    combined = dot(spread, produced)
    return (mixed_ref[...].astype(F32) + info_ref[:, 0:1] * combined).astype(BF16)


def combine_kernel(mixed_ref, info_ref, _, *refs):
    *piece_refs, north_ref, own_ref, corner_ref, east_ref = refs
    state = gathered_state(mixed_ref, info_ref, piece_refs).astype(F32)
    low, high = split_halves(state)
    edge = east_ref.shape[0]
    north_ref[...] = low.astype(BF16)
    own_ref[...] = high.astype(BF16)
    corner_ref[...] = low[:edge].astype(BF16)
    east_ref[...] = high[:edge].astype(BF16)


def last_kernel(mixed_ref, info_ref, order, *refs):
    *piece_refs, out_ref = refs
    state = gathered_state(mixed_ref, info_ref, piece_refs)
    out_ref[...] = dot(one_hot_rows(order.get(), out_ref.shape[0]), state).astype(BF16)


SCALARS = pl.BlockSpec(memory_space=pltpu.SMEM)
IN_HBM = pl.BlockSpec(memory_space=pltpu.HBM)
IN_VMEM = pl.BlockSpec(memory_space=pltpu.VMEM)
UNREAD = "unread"


def keep_out(array):
    return pltpu.with_memory_space_constraint(array, pltpu.HBM)


def call(kernel, ins, outs, scratch=(), limit=40, flops=0):
    arrays, specs, rooms = [], [], []
    for array, how in ins:
        specs.append(how if how in (SCALARS, IN_VMEM) else IN_HBM)
        arrays.append(array if how == IN_VMEM else keep_out(array))
        if isinstance(how, tuple):
            rooms.append(pltpu.VMEM(array.shape[len(how) :], array.dtype))
    brought = len(rooms)

    def body(*refs):
        operands = list(refs[: len(ins)])
        room_refs, arrived = (refs[-1 - brought : -1], refs[-1]) if brought else ((), None)
        others = refs[len(ins) : len(refs) - (brought + 1 if brought else 0)]
        at = 0
        for index, (_, how) in enumerate(ins):
            if isinstance(how, tuple):
                source = operands[index].at[how] if how else operands[index]
                operands[index] = Brought(source, room_refs[at], arrived.at[at])
                at += 1
        kernel(*operands, *others)

    size = sum(a.size * a.dtype.itemsize for a in arrays)
    return pl.pallas_call(
        body,
        in_specs=specs,
        out_specs=[IN_VMEM] * len(outs),
        out_shape=outs,
        scratch_shapes=list(scratch) + rooms + ([pltpu.SemaphoreType.DMA((brought,))] if brought else []),
        compiler_params=pltpu.CompilerParams(vmem_limit_bytes=limit * MIB),
        cost_estimate=pl.CostEstimate(flops=flops, bytes_accessed=size, transcendentals=0),
    )(*arrays)


def run_near(piece, weights, plan, base, layer):
    channels, units = piece.shape[1], weights[0].shape[3]
    held = [pltpu.VMEM((len(plan), channels, units), BF16), pltpu.VMEM((len(plan), units, channels), BF16)]
    out, *held = pl.pallas_call(
        functools.partial(near_kernel, plan=plan, base=base, layer=layer),
        in_specs=[IN_VMEM] + [IN_HBM] * len(weights),
        out_specs=[IN_VMEM] * 3,
        out_shape=[jax.ShapeDtypeStruct(piece.shape, BF16)] + held,
        scratch_shapes=[pltpu.SemaphoreType.DMA((2, len(plan)))],
        compiler_params=pltpu.CompilerParams(vmem_limit_bytes=24 * MIB),
        cost_estimate=pl.CostEstimate(
            flops=3_000_000_000, bytes_accessed=len(plan) * 4 * channels * units, transcendentals=0
        ),
    )(piece, *[keep_out(w) for w in weights])
    return out, held


def run_away(whole, cut, held, plan, base, kept):
    pieces = whole + cut
    channels = pieces[0].shape[1]
    size = (max(place for _, _, place in plan) - base + 1) * CAP
    sizes = [size + rows.shape[0] for rows in kept] + [size] * (len(pieces) - len(kept))
    return pl.pallas_call(
        functools.partial(away_kernel, whole=len(whole), cut=len(cut), plan=plan, base=base, kept=len(kept)),
        in_specs=[IN_VMEM] * (len(pieces) + 2 + len(kept)),
        out_specs=[IN_VMEM] * len(pieces),
        out_shape=[jax.ShapeDtypeStruct((rows, channels), BF16) for rows in sizes],
        compiler_params=pltpu.CompilerParams(vmem_limit_bytes=24 * MIB),
        cost_estimate=pl.CostEstimate(flops=3_000_000_000, bytes_accessed=1 << 20, transcendentals=0),
    )(*pieces, *held, *kept)


def lat_lon_pairs(lat_step, lon_step):
    bands, sectors = lax.axis_size("lat"), lax.axis_size("lon")
    pairs = []
    for i in range(bands):
        for j in range(sectors):
            target = (i + lat_step) % bands * sectors + (j + lon_step) % sectors
            pairs.append((i * sectors + j, target))
    return pairs


def shift(value, lat_step, lon_step):
    return lax.ppermute(value, ("lat", "lon"), lat_lon_pairs(lat_step, lon_step))


def between(value, distance):
    sectors = lax.axis_size("lon")
    return lax.ppermute(value, "lon", [(s, s ^ distance) for s in range(sectors)])


def per_device(tokens, expert_ids, norm_gain, weight_qkv, weight_proj, temper, router, weight_in, weight_out):
    row_count, col_count, channels = tokens.shape
    token_count = row_count * col_count
    half = token_count // 2
    strip = HALF * HALF
    part = WIN * HALF
    edge = 48
    sectors = lax.axis_size("lon")
    local = weight_in.shape[1]
    pieces_count = sectors // 2
    pair_experts = EXPERTS // pieces_count
    slots = pair_experts * CAP
    lon = lax.axis_index("lon")
    lat = lax.axis_index("lat")

    far_in = between(weight_in, 1)
    far_out = between(weight_out, 1)

    router = router.transpose(0, 2, 1)
    ids = expert_ids.reshape(LAYERS, 1, token_count)
    seam = jnp.where(lat == lax.axis_size("lat") - 1, 1, 0)
    place = jnp.stack([seam, lon // 2, lon % 2]).astype(jnp.int32).reshape(1, 3)

    grid = np.arange(token_count, dtype=np.int32).reshape(row_count // HALF, HALF, col_count // HALF, HALF)
    halves = grid.transpose(0, 2, 1, 3).reshape(2, half)
    order0 = halves.reshape(2, half // part, part).transpose(1, 0, 2).reshape(token_count)
    gap = np.full(strip, -1, np.int32)
    lead = np.full(edge - strip, -1, np.int32)
    low, high = halves
    order1 = np.concatenate([high[strip:], gap, low[strip:], gap, lead, high[:strip], lead, low[:strip]])
    rows1 = order1.shape[0]
    order0, order1 = jnp.asarray(order0)[None], jnp.asarray(order1)[None]

    shape = jax.ShapeDtypeStruct
    chunks = 2 if local > 1 else 1
    piece_shapes = [shape((rows, channels), BF16) for rows in piece_sizes(pieces_count, slots, chunks)]
    attention_scratch = [
        pltpu.VMEM((token_count, 3 * channels), BF16), pltpu.VMEM((token_count, channels), BF16),
    ]

    layer = 0
    mixed, info, *pieces = call(
        functools.partial(first_kernel, layer=layer, pair_experts=pair_experts),
        [(place, SCALARS), (temper, SCALARS), (tokens.reshape(token_count, channels), ()),
         (order0, ()), (ids, (layer,)),
         (norm_gain, (layer,)), (weight_qkv, (layer,)), (weight_proj, (layer,)), (router, (layer,))],
        [shape((token_count, channels), BF16), shape((token_count, 2), F32)] + piece_shapes,
        attention_scratch,
        flops=4_000_000_000,
    )
    columns1, row1, wqkv1, wproj1 = call(
        functools.partial(ahead_kernel, layer=1, pair_experts=pair_experts),
        [(place, SCALARS), (ids, (1,)), (order1, ()), (weight_qkv, UNREAD), (weight_proj, UNREAD), (info, IN_VMEM)],
        [shape((rows1, 2), F32), shape((1, rows1), F32),
         pltpu.VMEM((channels, 3 * channels), BF16), pltpu.VMEM((channels, channels), BF16)],
        [pltpu.SemaphoreType.DMA((2,))],
        flops=2_000_000_000,
    )
    produced = moe(pieces, pieces_count, weight_in, weight_out, far_in, far_out, layer)
    north, own, corner, east = call(
        combine_kernel,
        [(mixed, IN_VMEM), (info, IN_VMEM), (row1, IN_VMEM)] + [(p, IN_VMEM) for p in produced],
        [shape((half, channels), BF16)] * 2 + [shape((edge, channels), BF16)] * 2,
        flops=1_000_000_000,
    )

    layer = 1
    north = shift(north, -1, 0)
    east = shift(east, 0, -1)
    corner = shift(corner, -1, -1)
    low, high, low_edge, high_edge = call(
        functools.partial(shifted_kernel, layer=layer),
        [(place, SCALARS), (temper, SCALARS), (own, IN_VMEM), (north, IN_VMEM), (east, IN_VMEM), (corner, IN_VMEM),
         (norm_gain, (layer,)), (wqkv1, IN_VMEM), (wproj1, IN_VMEM)],
        [shape((half, channels), BF16)] * 2 + [shape((edge, channels), BF16)] * 2,
        [pltpu.VMEM((half + edge, channels), F32)] * 2 + attention_scratch,
        flops=3_000_000_000,
    )
    high = shift(high, 1, 0)
    low_edge = shift(low_edge, 0, 1)
    high_edge = shift(high_edge, 1, 1)
    mixed, info, *pieces = call(
        route_kernel,
        [(low, IN_VMEM), (high, IN_VMEM), (low_edge, IN_VMEM), (high_edge, IN_VMEM), (columns1, IN_VMEM),
         (row1, IN_VMEM), (norm_gain, (layer,)), (router, (layer,))],
        [shape((rows1, channels), BF16), shape((rows1, 2), F32)] + piece_shapes,
        flops=1_000_000_000,
    )
    produced = moe(pieces, pieces_count, weight_in, weight_out, far_in, far_out, layer)
    (out,) = call(
        last_kernel,
        [(mixed, IN_VMEM), (info, IN_VMEM), (order1, ())] + [(p, IN_VMEM) for p in produced],
        [shape((token_count, channels), BF16)],
        flops=1_000_000_000,
    )
    return out.reshape(row_count, col_count, channels)


def after(value, done):
    return lax.optimization_barrier((value, done))[0]


def in_chunks(count, k):
    return k == 0 or k >= count // 2


def piece_sizes(count, slots, chunks):
    return [n for k in range(count) for n in ([slots // chunks] * chunks if in_chunks(count, k) else [slots])]


def moe(flat, count, own_in, own_out, far_in, far_out, layer):
    local = own_in.shape[1]
    if local > 1:
        half = local // 2
        turns = [
            ([own_in, own_out], [(0, entry, entry // 2) for entry in range(local)], 0),
            ([far_in, far_out], [(0, entry, half + entry // 2) for entry in range(local)], half),
        ]
    else:
        turns = [([own_in, own_out, far_in, far_out], [(0, 0, 0), (1, 0, 0)], 0)]
    rest = iter(flat)
    pieces = [[next(rest) for _ in turns] if in_chunks(count, k) else next(rest) for k in range(count)]
    away = [k for k in range(1, count) if in_chunks(count, k)]
    beside = [k for k in range(1, count) if not in_chunks(count, k)]
    own, held, arrived, whole = [], [], [], None
    for turn, (weights, plan, base) in enumerate(turns):
        sent = [pieces[k][turn] for k in away]
        if own:
            sent = [after(value, own[-1]) for value in sent]
        arrived.append([between(value, 2 * k) for k, value in zip(away, sent)])
        if whole is None:
            whole = [between(pieces[k], 2 * k) for k in beside]
        piece = pieces[0][turn]
        if own:
            piece = after((piece, sent), own[-1])[0]
        out, weights_here = run_near(piece, weights, plan, base, layer)
        own.append(out)
        held.append(weights_here)
    back = {k: [] for k in away}
    kept = []
    for turn, (_, plan, base) in enumerate(turns):
        outs = run_away(whole, arrived[turn], held[turn], plan, base, kept)
        kept = outs[: len(whole)]
        for k, value in zip(away, outs[len(whole) :]):
            if back[k]:
                value = after(value, back[k][-1])
            back[k].append(between(value, 2 * k))
    back[0] = own
    for k, value in zip(beside, kept):
        back[k] = [between(value, 2 * k)]
    return [value for k in range(count) for value in back[k]]


def solution(mesh):
    in_specs = (
        P("lat", "lon", None),
        P(None, "lat", "lon", None, None),
        P(),
        P(),
        P(),
        P(),
        P(),
        P(None, "lon", None, None),
        P(None, "lon", None, None),
    )
    out_specs = P("lat", "lon", None)
    return jax.shard_map(per_device, mesh=mesh, in_specs=in_specs, out_specs=out_specs, check_vma=False)
```

```python
import functools
import math

import jax
import jax.numpy as jnp
import numpy as np
from jax import lax
from jax.experimental import pallas as pl
from jax.experimental.pallas import tpu as pltpu
from jax.sharding import PartitionSpec as P

WIN = 12
HALF = WIN // 2
EXPERTS = 16
LAYERS = 2
CAP = 48
EPSILON = 1e-05
LANES = 128
MIB = 1 << 20

F32 = jnp.float32
BF16 = jnp.bfloat16


def norm_rows(values, gain_row):
    centered = values - jnp.mean(values, axis=-1, keepdims=True)
    variance = jnp.mean(centered * centered, axis=-1, keepdims=True)
    return (centered * lax.rsqrt(variance + EPSILON) * gain_row).astype(BF16)


def dot(left, right, dims=((1,), (0,))):
    return lax.dot_general(left, right, (dims, ((), ())), preferred_element_type=F32)


def one_hot_columns(column, count):
    spread = lax.broadcasted_iota(jnp.int32, (column.shape[0], count), 1)
    return jnp.where(spread == column, 1.0, 0.0).astype(BF16)


def one_hot_rows(row, count):
    spread = lax.broadcasted_iota(jnp.int32, (count, row.shape[1]), 0)
    return jnp.where(spread == row, 1.0, 0.0).astype(BF16)


class Brought:
    def __init__(self, source, target, arrived):
        self.target, self.pending = target, True
        self.copy = pltpu.make_async_copy(source, target, arrived)
        self.copy.start()

    def get(self):
        if self.pending:
            self.copy.wait()
            self.pending = False
        return self.target[...]


def upright(row):
    return jnp.transpose(jnp.broadcast_to(row.astype(F32), (LANES, row.shape[1])))


def slots_of(ids_row, reorder, place_ref, pair_experts):
    count = ids_row.shape[1]
    spread_ids = upright(ids_row).astype(jnp.int32)
    ids = spread_ids[:, 0:1]
    chosen = lax.broadcasted_iota(jnp.int32, (count, LANES), 1) == spread_ids
    earlier = lax.broadcasted_iota(jnp.int32, (count, count), 0) > lax.broadcasted_iota(jnp.int32, (count, count), 1)
    before = dot(jnp.where(earlier, 1.0, 0.0).astype(BF16), jnp.where(chosen, 1.0, 0.0).astype(BF16))
    place = jnp.sum(jnp.where(chosen, before, 0.0), axis=1, keepdims=True).astype(jnp.int32)
    shift_by = pair_experts.bit_length() - 1
    piece = (ids >> shift_by) ^ place_ref[0, 1]
    inner = (ids & (pair_experts - 1)) ^ (place_ref[0, 2] * (pair_experts // 2))
    target = (piece * pair_experts + inner) * CAP + place
    lane = lax.broadcasted_iota(jnp.int32, (count, LANES), 1)
    parts = jnp.where(lane == 0, target >> 8, jnp.where(lane == 1, target & 255, jnp.where(lane == 2, ids, 1)))
    moved = dot(reorder, parts.astype(F32).astype(BF16))
    slot = jnp.where(moved[:, 3:4] > 0.5, moved[:, 0:1] * 256.0 + moved[:, 1:2], -1.0)
    row = jnp.transpose(jnp.broadcast_to(slot, (slot.shape[0], LANES)))[0:1, :]
    return moved[:, 2:3], slot, row


def route(ynorm, router, experts, target_row, piece_refs):
    logits = dot(ynorm, router, ((1,), (1,)))
    chosen = lax.broadcasted_iota(jnp.int32, logits.shape, 1) == experts.astype(jnp.int32)
    picked = jnp.sum(jnp.where(chosen, logits, 0.0), axis=1, keepdims=True)
    target = target_row.astype(jnp.int32)
    placed = dot(one_hot_rows(target, sum(ref.shape[0] for ref in piece_refs)), ynorm)
    start = 0
    for piece_ref in piece_refs:
        slots = piece_ref.shape[0]
        piece_ref[...] = placed[start : start + slots].astype(BF16)
        start += slots
    return jax.nn.sigmoid(picked)


def attend(frame, layer, place_ref, temper_ref, gain, wqkv, wproj, qkv_ref, context_ref):
    total, channels = frame.shape
    heads = temper_ref.shape[1]
    width = channels // heads
    area = WIN * WIN
    windows = total // area
    group = LANES // width
    main = LANES
    rest = area - main
    lanes = group * area
    normed = norm_rows(frame, gain.get()[0:1, :])
    qkv_ref[...] = dot(normed, wqkv()).astype(BF16)

    lane = lax.broadcasted_iota(jnp.int32, (1, lanes), 1)
    leftover = lane >= group * main
    head_of = jnp.where(leftover, (lane - group * main) // rest, lane // main)
    query_of = jnp.where(leftover, main + (lane - group * main) % rest, lane % main)
    late = query_of >= area // 2
    seam = place_ref[0, 0] > 0
    bias_early = jnp.where(jnp.logical_and(seam, late), -1e30, 0.0)
    bias_late = jnp.where(jnp.logical_and(seam, jnp.logical_not(late)), -1e30, 0.0)
    channel_head = lax.broadcasted_iota(jnp.int32, (1, LANES), 1) // width
    keep = [jnp.where(channel_head == h, 1.0, 0.0).astype(BF16) for h in range(group)]
    keep_f = [jnp.where(channel_head == h, 1.0, 0.0) for h in range(group)]

    def one_window(window):
        rows = pl.ds(window * area, area)
        for g in range(channels // LANES):
            q = qkv_ref[rows, g * LANES : (g + 1) * LANES]
            k = qkv_ref[rows, channels + g * LANES : channels + (g + 1) * LANES]
            v = qkv_ref[rows, 2 * channels + g * LANES : 2 * channels + (g + 1) * LANES]
            stacked = jnp.concatenate(
                [q[:main] * keep[h] for h in range(group)] + [q[main:] * keep[h] for h in range(group)], axis=0
            )
            scores = dot(k, stacked, ((1,), (1,)))
            scale = jnp.zeros((1, lanes), F32)
            for h in range(group):
                factor = temper_ref[layer, g * group + h] * (math.log2(math.e) / math.sqrt(width))
                scale = jnp.where(head_of == h, factor, scale)
            if layer % 2 == 1:
                scores = jnp.concatenate(
                    [scores[: area // 2] + bias_early, scores[area // 2 :] + bias_late], axis=0
                )
            peak = jnp.max(scores, axis=0, keepdims=True)
            weights = jnp.exp2((scores - peak) * scale)
            inverse = 1.0 / jnp.sum(weights, axis=0, keepdims=True)
            mixed_t = dot(v, weights.astype(BF16), ((0,), (0,))) * inverse
            picked = jnp.concatenate(
                [mixed_t[h * width : (h + 1) * width, h * main : (h + 1) * main] for h in range(group)], axis=0
            )
            first = jnp.transpose(picked)
            tail = jnp.transpose(mixed_t[:, group * main :])
            second = tail[:rest] * keep_f[0]
            for h in range(1, group):
                second = second + tail[h * rest : (h + 1) * rest] * keep_f[h]
            context = jnp.concatenate([first, second], axis=0).astype(BF16)
            context_ref[rows, g * LANES : (g + 1) * LANES] = context

    for window in range(windows):
        one_window(window)
    attended = dot(context_ref[...], wproj())
    return (frame + attended).astype(BF16)


def first_kernel(
    place_ref, temper_ref, tokens, order, ids, gain, wqkv, wproj, router,
    mixed_ref, info_ref, *refs, layer, pair_experts
):
    *piece_refs, qkv_ref, context_ref = refs
    reorder = one_hot_columns(upright(order.get())[:, 0:1].astype(jnp.int32), order.target.shape[1])
    experts, slot, slot_row = slots_of(ids.get(), reorder, place_ref, pair_experts)
    frame = dot(reorder, tokens.get())
    mixed = attend(frame, layer, place_ref, temper_ref, gain, wqkv.get, wproj.get, qkv_ref, context_ref)
    mixed_ref[...] = mixed
    ynorm = norm_rows(mixed.astype(F32), gain.get()[1:2, :])
    gate = route(ynorm, router.get(), experts, slot_row, piece_refs)
    info_ref[...] = jnp.concatenate([gate, slot], axis=1)


def ahead_kernel(place_ref, ids, order, wqkv_hbm, wproj_hbm, _, columns_ref, row_ref, wqkv_ref, wproj_ref, arrived,
                 *, layer, pair_experts):
    copies = [
        pltpu.make_async_copy(source.at[layer], target, arrived.at[index])
        for index, (source, target) in enumerate(((wqkv_hbm, wqkv_ref), (wproj_hbm, wproj_ref)))
    ]
    for copy in copies:
        copy.start()
    ids_row = ids.get()
    reorder = one_hot_columns(upright(order.get())[:, 0:1].astype(jnp.int32), ids_row.shape[1])
    experts, slot, slot_row = slots_of(ids_row, reorder, place_ref, pair_experts)
    columns_ref[...] = jnp.concatenate([experts, slot], axis=1)
    row_ref[...] = slot_row
    for copy in copies:
        copy.wait()


def shifted_kernel(
    place_ref, temper_ref, own_ref, north_ref, east_ref, corner_ref, gain, wqkv_ref, wproj_ref,
    low_ref, high_ref, low_edge_ref, high_edge_ref,
    low_scratch, high_scratch, qkv_ref, context_ref, *, layer
):
    half, channels = own_ref.shape
    strip = HALF * HALF
    part = WIN * HALF
    edge = east_ref.shape[0]
    low_scratch[0:half] = own_ref[...].astype(F32)
    low_scratch[half : half + edge] = east_ref[...].astype(F32)
    high_scratch[0:half] = north_ref[...].astype(F32)
    high_scratch[half : half + edge] = corner_ref[...].astype(F32)
    pieces = []
    for window in range(half // part):
        start = strip + window * part
        pieces += [low_scratch[start : start + part], high_scratch[start : start + part]]
    frame = jnp.concatenate(pieces, axis=0)
    mixed = attend(
        frame, layer, place_ref, temper_ref, gain, lambda: wqkv_ref[...], lambda: wproj_ref[...], qkv_ref, context_ref
    )
    mixed = mixed.astype(F32)
    low, high = split_halves(mixed)
    low_ref[...] = low.astype(BF16)
    high_ref[...] = high.astype(BF16)
    low_edge_ref[...] = low[half - edge :].astype(BF16)
    high_edge_ref[...] = high[half - edge :].astype(BF16)


def split_halves(rows):
    part = WIN * HALF
    pieces = [rows[start : start + part] for start in range(0, rows.shape[0], part)]
    return jnp.concatenate(pieces[0::2], axis=0), jnp.concatenate(pieces[1::2], axis=0)


def route_kernel(own_ref, south_ref, west_ref, corner_ref, columns_ref, row_ref, gain, router,
                 rows_ref, info_ref, *piece_refs):
    mixed = jnp.concatenate([own_ref[...], south_ref[...], west_ref[...], corner_ref[...]], axis=0)
    rows_ref[...] = mixed
    ynorm = norm_rows(mixed.astype(F32), gain.get()[1:2, :])
    gate = route(ynorm, router.get(), columns_ref[:, 0:1], row_ref[...], piece_refs)
    info_ref[...] = jnp.concatenate([gate, columns_ref[:, 1:2]], axis=1)


def expert_rows(piece_refs, starts, out_refs, first, second, carried, last):
    rows = jnp.concatenate([ref[start : start + CAP, :] for ref, start in zip(piece_refs, starts)], axis=0)
    hidden = jax.nn.gelu(dot(rows, first())).astype(BF16)
    part = dot(hidden, second())
    total = part if carried is None else carried + part
    if last:
        for index, (ref, start) in enumerate(out_refs):
            ref[start : start + CAP, :] = total[index * CAP : (index + 1) * CAP].astype(BF16)
    return total


def near_kernel(*refs, plan, base, layer):
    piece_ref = refs[0]
    weights = refs[1:-4]
    out_ref, first_ref, second_ref, arrived = refs[-4:]
    ahead = 2
    copies = {}

    def begin(unit):
        if unit < len(plan):
            which, entry, _ = plan[unit]
            for side, target in enumerate((first_ref, second_ref)):
                copies[unit, side] = pltpu.make_async_copy(
                    weights[2 * which + side].at[layer, entry], target.at[unit], arrived.at[side, unit]
                )
                copies[unit, side].start()

    def wait_for(unit, side, ref):
        copies[unit, side].wait()
        if side == 0:
            begin(unit + ahead)
        return ref[unit]

    for unit in range(ahead):
        begin(unit)
    totals = {}
    last = {place: unit for unit, (_, _, place) in enumerate(plan)}
    for unit, (_, _, place) in enumerate(plan):
        start = (place - base) * CAP
        totals[place] = expert_rows(
            [piece_ref], [start], [(out_ref, start)],
            functools.partial(wait_for, unit, 0, first_ref), functools.partial(wait_for, unit, 1, second_ref),
            totals.get(place), last[place] == unit,
        )


def away_kernel(*refs, whole, cut, plan, base, kept):
    piece_refs = refs[: whole + cut]
    first_ref, second_ref = refs[whole + cut : whole + cut + 2]
    kept_refs = refs[whole + cut + 2 : whole + cut + 2 + kept]
    out_refs = refs[whole + cut + 2 + kept :]
    lead = [0] * (whole + cut)
    for index, ref in enumerate(kept_refs):
        lead[index] = ref.shape[0]
        out_refs[index][0 : lead[index], :] = ref[...]
    totals = {}
    last = {place: unit for unit, (_, _, place) in enumerate(plan)}
    for unit, (_, _, place) in enumerate(plan):
        inner = (place - base) * CAP
        totals[place] = expert_rows(
            piece_refs, [place * CAP] * whole + [inner] * cut,
            [(ref, start + inner) for ref, start in zip(out_refs, lead)],
            lambda unit=unit: first_ref[unit], lambda unit=unit: second_ref[unit],
            totals.get(place), last[place] == unit,
        )


def gathered_state(mixed_ref, info_ref, piece_refs):
    produced = jnp.concatenate([ref[...] for ref in piece_refs], axis=0)
    spread = one_hot_columns(info_ref[:, 1:2].astype(jnp.int32), produced.shape[0])
    combined = dot(spread, produced)
    return (mixed_ref[...].astype(F32) + info_ref[:, 0:1] * combined).astype(BF16)


def combine_kernel(mixed_ref, info_ref, _, *refs):
    *piece_refs, north_ref, own_ref, corner_ref, east_ref = refs
    state = gathered_state(mixed_ref, info_ref, piece_refs).astype(F32)
    low, high = split_halves(state)
    edge = east_ref.shape[0]
    north_ref[...] = low.astype(BF16)
    own_ref[...] = high.astype(BF16)
    corner_ref[...] = low[:edge].astype(BF16)
    east_ref[...] = high[:edge].astype(BF16)


def last_kernel(mixed_ref, info_ref, order, *refs):
    *piece_refs, out_ref = refs
    state = gathered_state(mixed_ref, info_ref, piece_refs)
    out_ref[...] = dot(one_hot_rows(order.get(), out_ref.shape[0]), state).astype(BF16)


SCALARS = pl.BlockSpec(memory_space=pltpu.SMEM)
IN_HBM = pl.BlockSpec(memory_space=pltpu.HBM)
IN_VMEM = pl.BlockSpec(memory_space=pltpu.VMEM)
UNREAD = "unread"


def keep_out(array):
    return pltpu.with_memory_space_constraint(array, pltpu.HBM)


def call(kernel, ins, outs, scratch=(), limit=40, flops=0):
    arrays, specs, rooms = [], [], []
    for array, how in ins:
        specs.append(how if how in (SCALARS, IN_VMEM) else IN_HBM)
        arrays.append(array if how == IN_VMEM else keep_out(array))
        if isinstance(how, tuple):
            rooms.append(pltpu.VMEM(array.shape[len(how) :], array.dtype))
    brought = len(rooms)

    def body(*refs):
        operands = list(refs[: len(ins)])
        room_refs, arrived = (refs[-1 - brought : -1], refs[-1]) if brought else ((), None)
        others = refs[len(ins) : len(refs) - (brought + 1 if brought else 0)]
        at = 0
        for index, (_, how) in enumerate(ins):
            if isinstance(how, tuple):
                source = operands[index].at[how] if how else operands[index]
                operands[index] = Brought(source, room_refs[at], arrived.at[at])
                at += 1
        kernel(*operands, *others)

    size = sum(a.size * a.dtype.itemsize for a in arrays)
    return pl.pallas_call(
        body,
        in_specs=specs,
        out_specs=[IN_VMEM] * len(outs),
        out_shape=outs,
        scratch_shapes=list(scratch) + rooms + ([pltpu.SemaphoreType.DMA((brought,))] if brought else []),
        compiler_params=pltpu.CompilerParams(vmem_limit_bytes=limit * MIB),
        cost_estimate=pl.CostEstimate(flops=flops, bytes_accessed=size, transcendentals=0),
    )(*arrays)


def run_near(piece, weights, plan, base, layer):
    channels, units = piece.shape[1], weights[0].shape[3]
    held = [pltpu.VMEM((len(plan), channels, units), BF16), pltpu.VMEM((len(plan), units, channels), BF16)]
    out, *held = pl.pallas_call(
        functools.partial(near_kernel, plan=plan, base=base, layer=layer),
        in_specs=[IN_VMEM] + [IN_HBM] * len(weights),
        out_specs=[IN_VMEM] * 3,
        out_shape=[jax.ShapeDtypeStruct(piece.shape, BF16)] + held,
        scratch_shapes=[pltpu.SemaphoreType.DMA((2, len(plan)))],
        compiler_params=pltpu.CompilerParams(vmem_limit_bytes=24 * MIB),
        cost_estimate=pl.CostEstimate(
            flops=3_000_000_000, bytes_accessed=len(plan) * 4 * channels * units, transcendentals=0
        ),
    )(piece, *[keep_out(w) for w in weights])
    return out, held


def run_away(whole, cut, held, plan, base, kept):
    pieces = whole + cut
    channels = pieces[0].shape[1]
    size = (max(place for _, _, place in plan) - base + 1) * CAP
    sizes = [size + rows.shape[0] for rows in kept] + [size] * (len(pieces) - len(kept))
    return pl.pallas_call(
        functools.partial(away_kernel, whole=len(whole), cut=len(cut), plan=plan, base=base, kept=len(kept)),
        in_specs=[IN_VMEM] * (len(pieces) + 2 + len(kept)),
        out_specs=[IN_VMEM] * len(pieces),
        out_shape=[jax.ShapeDtypeStruct((rows, channels), BF16) for rows in sizes],
        compiler_params=pltpu.CompilerParams(vmem_limit_bytes=24 * MIB),
        cost_estimate=pl.CostEstimate(flops=3_000_000_000, bytes_accessed=1 << 20, transcendentals=0),
    )(*pieces, *held, *kept)


def lat_lon_pairs(lat_step, lon_step):
    bands, sectors = lax.axis_size("lat"), lax.axis_size("lon")
    pairs = []
    for i in range(bands):
        for j in range(sectors):
            target = (i + lat_step) % bands * sectors + (j + lon_step) % sectors
            pairs.append((i * sectors + j, target))
    return pairs


def shift(value, lat_step, lon_step):
    return lax.ppermute(value, ("lat", "lon"), lat_lon_pairs(lat_step, lon_step))


def between(value, distance):
    sectors = lax.axis_size("lon")
    return lax.ppermute(value, "lon", [(s, s ^ distance) for s in range(sectors)])


def per_device(tokens, expert_ids, norm_gain, weight_qkv, weight_proj, temper, router, weight_in, weight_out):
    row_count, col_count, channels = tokens.shape
    token_count = row_count * col_count
    half = token_count // 2
    strip = HALF * HALF
    part = WIN * HALF
    edge = 48
    sectors = lax.axis_size("lon")
    local = weight_in.shape[1]
    pieces_count = sectors // 2
    pair_experts = EXPERTS // pieces_count
    slots = pair_experts * CAP
    lon = lax.axis_index("lon")
    lat = lax.axis_index("lat")

    far_in = between(weight_in, 1)
    far_out = between(weight_out, 1)

    router = router.transpose(0, 2, 1)
    ids = expert_ids.reshape(LAYERS, 1, token_count)
    seam = jnp.where(lat == lax.axis_size("lat") - 1, 1, 0)
    place = jnp.stack([seam, lon // 2, lon % 2]).astype(jnp.int32).reshape(1, 3)

    grid = np.arange(token_count, dtype=np.int32).reshape(row_count // HALF, HALF, col_count // HALF, HALF)
    halves = grid.transpose(0, 2, 1, 3).reshape(2, half)
    order0 = halves.reshape(2, half // part, part).transpose(1, 0, 2).reshape(token_count)
    gap = np.full(strip, -1, np.int32)
    lead = np.full(edge - strip, -1, np.int32)
    low, high = halves
    order1 = np.concatenate([high[strip:], gap, low[strip:], gap, lead, high[:strip], lead, low[:strip]])
    rows1 = order1.shape[0]
    order0, order1 = jnp.asarray(order0)[None], jnp.asarray(order1)[None]

    shape = jax.ShapeDtypeStruct
    chunks = 2 if local > 1 else 1
    piece_shapes = [shape((rows, channels), BF16) for rows in piece_sizes(pieces_count, slots, chunks)]
    attention_scratch = [
        pltpu.VMEM((token_count, 3 * channels), BF16), pltpu.VMEM((token_count, channels), BF16),
    ]

    layer = 0
    mixed, info, *pieces = call(
        functools.partial(first_kernel, layer=layer, pair_experts=pair_experts),
        [(place, SCALARS), (temper, SCALARS), (tokens.reshape(token_count, channels), ()),
         (order0, ()), (ids, (layer,)),
         (norm_gain, (layer,)), (weight_qkv, (layer,)), (weight_proj, (layer,)), (router, (layer,))],
        [shape((token_count, channels), BF16), shape((token_count, 2), F32)] + piece_shapes,
        attention_scratch,
        flops=4_000_000_000,
    )
    columns1, row1, wqkv1, wproj1 = call(
        functools.partial(ahead_kernel, layer=1, pair_experts=pair_experts),
        [(place, SCALARS), (ids, (1,)), (order1, ()), (weight_qkv, UNREAD), (weight_proj, UNREAD), (info, IN_VMEM)],
        [shape((rows1, 2), F32), shape((1, rows1), F32),
         pltpu.VMEM((channels, 3 * channels), BF16), pltpu.VMEM((channels, channels), BF16)],
        [pltpu.SemaphoreType.DMA((2,))],
        flops=2_000_000_000,
    )
    produced = moe(pieces, pieces_count, weight_in, weight_out, far_in, far_out, layer)
    north, own, corner, east = call(
        combine_kernel,
        [(mixed, IN_VMEM), (info, IN_VMEM), (row1, IN_VMEM)] + [(p, IN_VMEM) for p in produced],
        [shape((half, channels), BF16)] * 2 + [shape((edge, channels), BF16)] * 2,
        flops=1_000_000_000,
    )

    layer = 1
    north = shift(north, -1, 0)
    east = shift(east, 0, -1)
    corner = shift(corner, -1, -1)
    low, high, low_edge, high_edge = call(
        functools.partial(shifted_kernel, layer=layer),
        [(place, SCALARS), (temper, SCALARS), (own, IN_VMEM), (north, IN_VMEM), (east, IN_VMEM), (corner, IN_VMEM),
         (norm_gain, (layer,)), (wqkv1, IN_VMEM), (wproj1, IN_VMEM)],
        [shape((half, channels), BF16)] * 2 + [shape((edge, channels), BF16)] * 2,
        [pltpu.VMEM((half + edge, channels), F32)] * 2 + attention_scratch,
        flops=3_000_000_000,
    )
    high = shift(high, 1, 0)
    low_edge = shift(low_edge, 0, 1)
    high_edge = shift(high_edge, 1, 1)
    mixed, info, *pieces = call(
        route_kernel,
        [(low, IN_VMEM), (high, IN_VMEM), (low_edge, IN_VMEM), (high_edge, IN_VMEM), (columns1, IN_VMEM),
         (row1, IN_VMEM), (norm_gain, (layer,)), (router, (layer,))],
        [shape((rows1, channels), BF16), shape((rows1, 2), F32)] + piece_shapes,
        flops=1_000_000_000,
    )
    produced = moe(pieces, pieces_count, weight_in, weight_out, far_in, far_out, layer)
    (out,) = call(
        last_kernel,
        [(mixed, IN_VMEM), (info, IN_VMEM), (order1, ())] + [(p, IN_VMEM) for p in produced],
        [shape((token_count, channels), BF16)],
        flops=1_000_000_000,
    )
    return out.reshape(row_count, col_count, channels)


def after(value, done):
    return lax.optimization_barrier((value, done))[0]


def in_chunks(count, k):
    return k == 0 or k >= count // 2


def piece_sizes(count, slots, chunks):
    return [n for k in range(count) for n in ([slots // chunks] * chunks if in_chunks(count, k) else [slots])]


def moe(flat, count, own_in, own_out, far_in, far_out, layer):
    local = own_in.shape[1]
    if local > 1:
        half = local // 2
        turns = [
            ([own_in, own_out], [(0, entry, entry // 2) for entry in range(local)], 0),
            ([far_in, far_out], [(0, entry, half + entry // 2) for entry in range(local)], half),
        ]
    else:
        turns = [([own_in, own_out, far_in, far_out], [(0, 0, 0), (1, 0, 0)], 0)]
    rest = iter(flat)
    pieces = [[next(rest) for _ in turns] if in_chunks(count, k) else next(rest) for k in range(count)]
    away = [k for k in range(1, count) if in_chunks(count, k)]
    beside = [k for k in range(1, count) if not in_chunks(count, k)]
    own, held, arrived, whole = [], [], [], None
    for turn, (weights, plan, base) in enumerate(turns):
        sent = [pieces[k][turn] for k in away]
        if own:
            sent = [after(value, own[-1]) for value in sent]
        arrived.append([between(value, 2 * k) for k, value in zip(away, sent)])
        if whole is None:
            whole = [between(pieces[k], 2 * k) for k in beside]
        piece = pieces[0][turn]
        if own:
            piece = after((piece, sent), own[-1])[0]
        out, weights_here = run_near(piece, weights, plan, base, layer)
        own.append(out)
        held.append(weights_here)
    back = {k: [] for k in away}
    kept = []
    for turn, (_, plan, base) in enumerate(turns):
        outs = run_away(whole, arrived[turn], held[turn], plan, base, kept)
        kept = outs[: len(whole)]
        for k, value in zip(away, outs[len(whole) :]):
            if back[k]:
                value = after(value, back[k][-1])
            back[k].append(between(value, 2 * k))
    back[0] = own
    for k, value in zip(beside, kept):
        back[k] = [between(value, 2 * k)]
    return [value for k in range(count) for value in back[k]]


def solution(mesh):
    in_specs = (
        P("lat", "lon", None),
        P(None, "lat", "lon", None, None),
        P(),
        P(),
        P(),
        P(),
        P(),
        P(None, "lon", None, None),
        P(None, "lon", None, None),
    )
    out_specs = P("lat", "lon", None)
    return jax.shard_map(per_device, mesh=mesh, in_specs=in_specs, out_specs=out_specs, check_vma=False)
```

```python
import functools
import math

import jax
import jax.numpy as jnp
import numpy as np
from jax import lax
from jax.experimental import pallas as pl
from jax.experimental.pallas import tpu as pltpu
from jax.sharding import PartitionSpec as P

WIN = 12
HALF = WIN // 2
EXPERTS = 16
LAYERS = 2
CAP = 48
EPSILON = 1e-05
LANES = 128
MIB = 1 << 20

F32 = jnp.float32
BF16 = jnp.bfloat16


def norm_rows(values, gain_row):
    centered = values - jnp.mean(values, axis=-1, keepdims=True)
    variance = jnp.mean(centered * centered, axis=-1, keepdims=True)
    return (centered * lax.rsqrt(variance + EPSILON) * gain_row).astype(BF16)


def dot(left, right, dims=((1,), (0,))):
    return lax.dot_general(left, right, (dims, ((), ())), preferred_element_type=F32)


def one_hot_columns(column, count):
    spread = lax.broadcasted_iota(jnp.int32, (column.shape[0], count), 1)
    return jnp.where(spread == column, 1.0, 0.0).astype(BF16)


def one_hot_rows(row, count):
    spread = lax.broadcasted_iota(jnp.int32, (count, row.shape[1]), 0)
    return jnp.where(spread == row, 1.0, 0.0).astype(BF16)


class Brought:
    def __init__(self, source, target, arrived):
        self.target, self.pending = target, True
        self.copy = pltpu.make_async_copy(source, target, arrived)
        self.copy.start()

    def get(self):
        if self.pending:
            self.copy.wait()
            self.pending = False
        return self.target[...]


def upright(row):
    return jnp.transpose(jnp.broadcast_to(row.astype(F32), (LANES, row.shape[1])))


def slots_of(ids_row, reorder, place_ref, pair_experts):
    count = ids_row.shape[1]
    spread_ids = upright(ids_row).astype(jnp.int32)
    ids = spread_ids[:, 0:1]
    chosen = lax.broadcasted_iota(jnp.int32, (count, LANES), 1) == spread_ids
    earlier = lax.broadcasted_iota(jnp.int32, (count, count), 0) > lax.broadcasted_iota(jnp.int32, (count, count), 1)
    before = dot(jnp.where(earlier, 1.0, 0.0).astype(BF16), jnp.where(chosen, 1.0, 0.0).astype(BF16))
    place = jnp.sum(jnp.where(chosen, before, 0.0), axis=1, keepdims=True).astype(jnp.int32)
    shift_by = pair_experts.bit_length() - 1
    piece = (ids >> shift_by) ^ place_ref[0, 1]
    inner = (ids & (pair_experts - 1)) ^ (place_ref[0, 2] * (pair_experts // 2))
    target = (piece * pair_experts + inner) * CAP + place
    lane = lax.broadcasted_iota(jnp.int32, (count, LANES), 1)
    parts = jnp.where(lane == 0, target >> 8, jnp.where(lane == 1, target & 255, jnp.where(lane == 2, ids, 1)))
    moved = dot(reorder, parts.astype(F32).astype(BF16))
    slot = jnp.where(moved[:, 3:4] > 0.5, moved[:, 0:1] * 256.0 + moved[:, 1:2], -1.0)
    row = jnp.transpose(jnp.broadcast_to(slot, (slot.shape[0], LANES)))[0:1, :]
    return moved[:, 2:3], slot, row


def route(ynorm, router, experts, target_row, piece_refs):
    logits = dot(ynorm, router, ((1,), (1,)))
    chosen = lax.broadcasted_iota(jnp.int32, logits.shape, 1) == experts.astype(jnp.int32)
    picked = jnp.sum(jnp.where(chosen, logits, 0.0), axis=1, keepdims=True)
    target = target_row.astype(jnp.int32)
    placed = dot(one_hot_rows(target, sum(ref.shape[0] for ref in piece_refs)), ynorm)
    start = 0
    for piece_ref in piece_refs:
        slots = piece_ref.shape[0]
        piece_ref[...] = placed[start : start + slots].astype(BF16)
        start += slots
    return jax.nn.sigmoid(picked)


def attend(frame, layer, place_ref, temper_ref, gain, wqkv, wproj, qkv_ref, context_ref):
    total, channels = frame.shape
    heads = temper_ref.shape[1]
    width = channels // heads
    area = WIN * WIN
    windows = total // area
    group = LANES // width
    main = LANES
    rest = area - main
    lanes = group * area
    normed = norm_rows(frame, gain.get()[0:1, :])
    qkv_ref[...] = dot(normed, wqkv()).astype(BF16)

    lane = lax.broadcasted_iota(jnp.int32, (1, lanes), 1)
    leftover = lane >= group * main
    head_of = jnp.where(leftover, (lane - group * main) // rest, lane // main)
    query_of = jnp.where(leftover, main + (lane - group * main) % rest, lane % main)
    late = query_of >= area // 2
    seam = place_ref[0, 0] > 0
    bias_early = jnp.where(jnp.logical_and(seam, late), -1e30, 0.0)
    bias_late = jnp.where(jnp.logical_and(seam, jnp.logical_not(late)), -1e30, 0.0)
    channel_head = lax.broadcasted_iota(jnp.int32, (1, LANES), 1) // width
    keep = [jnp.where(channel_head == h, 1.0, 0.0).astype(BF16) for h in range(group)]
    keep_f = [jnp.where(channel_head == h, 1.0, 0.0) for h in range(group)]

    def one_window(window):
        rows = pl.ds(window * area, area)
        for g in range(channels // LANES):
            q = qkv_ref[rows, g * LANES : (g + 1) * LANES]
            k = qkv_ref[rows, channels + g * LANES : channels + (g + 1) * LANES]
            v = qkv_ref[rows, 2 * channels + g * LANES : 2 * channels + (g + 1) * LANES]
            stacked = jnp.concatenate(
                [q[:main] * keep[h] for h in range(group)] + [q[main:] * keep[h] for h in range(group)], axis=0
            )
            scores = dot(k, stacked, ((1,), (1,)))
            scale = jnp.zeros((1, lanes), F32)
            for h in range(group):
                factor = temper_ref[layer, g * group + h] * (math.log2(math.e) / math.sqrt(width))
                scale = jnp.where(head_of == h, factor, scale)
            if layer % 2 == 1:
                scores = jnp.concatenate(
                    [scores[: area // 2] + bias_early, scores[area // 2 :] + bias_late], axis=0
                )
            peak = jnp.max(scores, axis=0, keepdims=True)
            weights = jnp.exp2((scores - peak) * scale)
            inverse = 1.0 / jnp.sum(weights, axis=0, keepdims=True)
            mixed_t = dot(v, weights.astype(BF16), ((0,), (0,))) * inverse
            picked = jnp.concatenate(
                [mixed_t[h * width : (h + 1) * width, h * main : (h + 1) * main] for h in range(group)], axis=0
            )
            first = jnp.transpose(picked.astype(BF16))
            tail = jnp.transpose(mixed_t[:, group * main :])
            second = tail[:rest] * keep_f[0]
            for h in range(1, group):
                second = second + tail[h * rest : (h + 1) * rest] * keep_f[h]
            context = jnp.concatenate([first, second.astype(BF16)], axis=0)
            context_ref[rows, g * LANES : (g + 1) * LANES] = context

    for window in range(windows):
        one_window(window)
    attended = dot(context_ref[...], wproj())
    return (frame + attended).astype(BF16)


def first_kernel(
    place_ref, temper_ref, tokens, order, ids, gain, wqkv, wproj, router,
    mixed_ref, info_ref, *refs, layer, pair_experts
):
    *piece_refs, qkv_ref, context_ref = refs
    reorder = one_hot_columns(upright(order.get())[:, 0:1].astype(jnp.int32), order.target.shape[1])
    experts, slot, slot_row = slots_of(ids.get(), reorder, place_ref, pair_experts)
    frame = dot(reorder, tokens.get())
    mixed = attend(frame, layer, place_ref, temper_ref, gain, wqkv.get, wproj.get, qkv_ref, context_ref)
    mixed_ref[...] = mixed
    ynorm = norm_rows(mixed.astype(F32), gain.get()[1:2, :])
    gate = route(ynorm, router.get(), experts, slot_row, piece_refs)
    info_ref[...] = jnp.concatenate([gate, slot], axis=1)


def ahead_kernel(place_ref, ids, order, wqkv_hbm, wproj_hbm, _, columns_ref, row_ref, wqkv_ref, wproj_ref, arrived,
                 *, layer, pair_experts):
    copies = [
        pltpu.make_async_copy(source.at[layer], target, arrived.at[index])
        for index, (source, target) in enumerate(((wqkv_hbm, wqkv_ref), (wproj_hbm, wproj_ref)))
    ]
    for copy in copies:
        copy.start()
    ids_row = ids.get()
    reorder = one_hot_columns(upright(order.get())[:, 0:1].astype(jnp.int32), ids_row.shape[1])
    experts, slot, slot_row = slots_of(ids_row, reorder, place_ref, pair_experts)
    columns_ref[...] = jnp.concatenate([experts, slot], axis=1)
    row_ref[...] = slot_row
    for copy in copies:
        copy.wait()


def shifted_kernel(
    place_ref, temper_ref, own_ref, north_ref, east_ref, corner_ref, gain, wqkv_ref, wproj_ref,
    low_ref, high_ref, low_edge_ref, high_edge_ref,
    low_scratch, high_scratch, qkv_ref, context_ref, *, layer
):
    half, channels = own_ref.shape
    strip = HALF * HALF
    part = WIN * HALF
    edge = east_ref.shape[0]
    low_scratch[0:half] = own_ref[...].astype(F32)
    low_scratch[half : half + edge] = east_ref[...].astype(F32)
    high_scratch[0:half] = north_ref[...].astype(F32)
    high_scratch[half : half + edge] = corner_ref[...].astype(F32)
    pieces = []
    for window in range(half // part):
        start = strip + window * part
        pieces += [low_scratch[start : start + part], high_scratch[start : start + part]]
    frame = jnp.concatenate(pieces, axis=0)
    mixed = attend(
        frame, layer, place_ref, temper_ref, gain, lambda: wqkv_ref[...], lambda: wproj_ref[...], qkv_ref, context_ref
    )
    mixed = mixed.astype(F32)
    low, high = split_halves(mixed)
    low_ref[...] = low.astype(BF16)
    high_ref[...] = high.astype(BF16)
    low_edge_ref[...] = low[half - edge :].astype(BF16)
    high_edge_ref[...] = high[half - edge :].astype(BF16)


def split_halves(rows):
    part = WIN * HALF
    pieces = [rows[start : start + part] for start in range(0, rows.shape[0], part)]
    return jnp.concatenate(pieces[0::2], axis=0), jnp.concatenate(pieces[1::2], axis=0)


def route_kernel(own_ref, south_ref, west_ref, corner_ref, columns_ref, row_ref, gain, router,
                 rows_ref, info_ref, *piece_refs):
    mixed = jnp.concatenate([own_ref[...], south_ref[...], west_ref[...], corner_ref[...]], axis=0)
    rows_ref[...] = mixed
    ynorm = norm_rows(mixed.astype(F32), gain.get()[1:2, :])
    gate = route(ynorm, router.get(), columns_ref[:, 0:1], row_ref[...], piece_refs)
    info_ref[...] = jnp.concatenate([gate, columns_ref[:, 1:2]], axis=1)


def expert_rows(piece_refs, starts, out_refs, first, second, carried, last):
    rows = jnp.concatenate([ref[start : start + CAP, :] for ref, start in zip(piece_refs, starts)], axis=0)
    hidden = jax.nn.gelu(dot(rows, first())).astype(BF16)
    part = dot(hidden, second())
    total = part if carried is None else carried + part
    if last:
        for index, (ref, start) in enumerate(out_refs):
            ref[start : start + CAP, :] = total[index * CAP : (index + 1) * CAP].astype(BF16)
    return total


def near_kernel(*refs, plan, base, layer):
    piece_ref = refs[0]
    weights = refs[1:-4]
    out_ref, first_ref, second_ref, arrived = refs[-4:]
    ahead = 2
    copies = {}

    def begin(unit):
        if unit < len(plan):
            which, entry, _ = plan[unit]
            for side, target in enumerate((first_ref, second_ref)):
                copies[unit, side] = pltpu.make_async_copy(
                    weights[2 * which + side].at[layer, entry], target.at[unit], arrived.at[side, unit]
                )
                copies[unit, side].start()

    def wait_for(unit, side, ref):
        copies[unit, side].wait()
        if side == 0:
            begin(unit + ahead)
        return ref[unit]

    for unit in range(ahead):
        begin(unit)
    totals = {}
    last = {place: unit for unit, (_, _, place) in enumerate(plan)}
    for unit, (_, _, place) in enumerate(plan):
        start = (place - base) * CAP
        totals[place] = expert_rows(
            [piece_ref], [start], [(out_ref, start)],
            functools.partial(wait_for, unit, 0, first_ref), functools.partial(wait_for, unit, 1, second_ref),
            totals.get(place), last[place] == unit,
        )


def away_kernel(*refs, whole, cut, plan, base, kept):
    piece_refs = refs[: whole + cut]
    first_ref, second_ref = refs[whole + cut : whole + cut + 2]
    kept_refs = refs[whole + cut + 2 : whole + cut + 2 + kept]
    out_refs = refs[whole + cut + 2 + kept :]
    lead = [0] * (whole + cut)
    for index, ref in enumerate(kept_refs):
        lead[index] = ref.shape[0]
        out_refs[index][0 : lead[index], :] = ref[...]
    totals = {}
    last = {place: unit for unit, (_, _, place) in enumerate(plan)}
    for unit, (_, _, place) in enumerate(plan):
        inner = (place - base) * CAP
        totals[place] = expert_rows(
            piece_refs, [place * CAP] * whole + [inner] * cut,
            [(ref, start + inner) for ref, start in zip(out_refs, lead)],
            lambda unit=unit: first_ref[unit], lambda unit=unit: second_ref[unit],
            totals.get(place), last[place] == unit,
        )


def gathered_state(mixed_ref, info_ref, piece_refs):
    produced = jnp.concatenate([ref[...] for ref in piece_refs], axis=0)
    spread = one_hot_columns(info_ref[:, 1:2].astype(jnp.int32), produced.shape[0])
    combined = dot(spread, produced)
    return (mixed_ref[...].astype(F32) + info_ref[:, 0:1] * combined).astype(BF16)


def combine_kernel(mixed_ref, info_ref, _, *refs):
    *piece_refs, north_ref, own_ref, corner_ref, east_ref = refs
    state = gathered_state(mixed_ref, info_ref, piece_refs).astype(F32)
    low, high = split_halves(state)
    edge = east_ref.shape[0]
    north_ref[...] = low.astype(BF16)
    own_ref[...] = high.astype(BF16)
    corner_ref[...] = low[:edge].astype(BF16)
    east_ref[...] = high[:edge].astype(BF16)


def last_kernel(mixed_ref, info_ref, order, *refs):
    *piece_refs, out_ref = refs
    state = gathered_state(mixed_ref, info_ref, piece_refs)
    out_ref[...] = dot(one_hot_rows(order.get(), out_ref.shape[0]), state).astype(BF16)


SCALARS = pl.BlockSpec(memory_space=pltpu.SMEM)
IN_HBM = pl.BlockSpec(memory_space=pltpu.HBM)
IN_VMEM = pl.BlockSpec(memory_space=pltpu.VMEM)
UNREAD = "unread"


def keep_out(array):
    return pltpu.with_memory_space_constraint(array, pltpu.HBM)


def call(kernel, ins, outs, scratch=(), limit=40, flops=0):
    arrays, specs, rooms = [], [], []
    for array, how in ins:
        specs.append(how if how in (SCALARS, IN_VMEM) else IN_HBM)
        arrays.append(array if how == IN_VMEM else keep_out(array))
        if isinstance(how, tuple):
            rooms.append(pltpu.VMEM(array.shape[len(how) :], array.dtype))
    brought = len(rooms)

    def body(*refs):
        operands = list(refs[: len(ins)])
        room_refs, arrived = (refs[-1 - brought : -1], refs[-1]) if brought else ((), None)
        others = refs[len(ins) : len(refs) - (brought + 1 if brought else 0)]
        at = 0
        for index, (_, how) in enumerate(ins):
            if isinstance(how, tuple):
                source = operands[index].at[how] if how else operands[index]
                operands[index] = Brought(source, room_refs[at], arrived.at[at])
                at += 1
        kernel(*operands, *others)

    size = sum(a.size * a.dtype.itemsize for a in arrays)
    return pl.pallas_call(
        body,
        in_specs=specs,
        out_specs=[IN_VMEM] * len(outs),
        out_shape=outs,
        scratch_shapes=list(scratch) + rooms + ([pltpu.SemaphoreType.DMA((brought,))] if brought else []),
        compiler_params=pltpu.CompilerParams(vmem_limit_bytes=limit * MIB),
        cost_estimate=pl.CostEstimate(flops=flops, bytes_accessed=size, transcendentals=0),
    )(*arrays)


def run_near(piece, weights, plan, base, layer):
    channels, units = piece.shape[1], weights[0].shape[3]
    held = [pltpu.VMEM((len(plan), channels, units), BF16), pltpu.VMEM((len(plan), units, channels), BF16)]
    out, *held = pl.pallas_call(
        functools.partial(near_kernel, plan=plan, base=base, layer=layer),
        in_specs=[IN_VMEM] + [IN_HBM] * len(weights),
        out_specs=[IN_VMEM] * 3,
        out_shape=[jax.ShapeDtypeStruct(piece.shape, BF16)] + held,
        scratch_shapes=[pltpu.SemaphoreType.DMA((2, len(plan)))],
        compiler_params=pltpu.CompilerParams(vmem_limit_bytes=24 * MIB),
        cost_estimate=pl.CostEstimate(
            flops=3_000_000_000, bytes_accessed=len(plan) * 4 * channels * units, transcendentals=0
        ),
    )(piece, *[keep_out(w) for w in weights])
    return out, held


def run_away(whole, cut, held, plan, base, kept):
    pieces = whole + cut
    channels = pieces[0].shape[1]
    size = (max(place for _, _, place in plan) - base + 1) * CAP
    sizes = [size + rows.shape[0] for rows in kept] + [size] * (len(pieces) - len(kept))
    return pl.pallas_call(
        functools.partial(away_kernel, whole=len(whole), cut=len(cut), plan=plan, base=base, kept=len(kept)),
        in_specs=[IN_VMEM] * (len(pieces) + 2 + len(kept)),
        out_specs=[IN_VMEM] * len(pieces),
        out_shape=[jax.ShapeDtypeStruct((rows, channels), BF16) for rows in sizes],
        compiler_params=pltpu.CompilerParams(vmem_limit_bytes=24 * MIB),
        cost_estimate=pl.CostEstimate(flops=3_000_000_000, bytes_accessed=1 << 20, transcendentals=0),
    )(*pieces, *held, *kept)


def lat_lon_pairs(lat_step, lon_step):
    bands, sectors = lax.axis_size("lat"), lax.axis_size("lon")
    pairs = []
    for i in range(bands):
        for j in range(sectors):
            target = (i + lat_step) % bands * sectors + (j + lon_step) % sectors
            pairs.append((i * sectors + j, target))
    return pairs


def shift(value, lat_step, lon_step):
    return lax.ppermute(value, ("lat", "lon"), lat_lon_pairs(lat_step, lon_step))


def between(value, distance):
    sectors = lax.axis_size("lon")
    return lax.ppermute(value, "lon", [(s, s ^ distance) for s in range(sectors)])


def per_device(tokens, expert_ids, norm_gain, weight_qkv, weight_proj, temper, router, weight_in, weight_out):
    row_count, col_count, channels = tokens.shape
    token_count = row_count * col_count
    half = token_count // 2
    strip = HALF * HALF
    part = WIN * HALF
    edge = 48
    sectors = lax.axis_size("lon")
    local = weight_in.shape[1]
    pieces_count = sectors // 2
    pair_experts = EXPERTS // pieces_count
    slots = pair_experts * CAP
    lon = lax.axis_index("lon")
    lat = lax.axis_index("lat")

    far_in = between(weight_in, 1)
    far_out = between(weight_out, 1)

    router = router.transpose(0, 2, 1)
    ids = expert_ids.reshape(LAYERS, 1, token_count)
    seam = jnp.where(lat == lax.axis_size("lat") - 1, 1, 0)
    place = jnp.stack([seam, lon // 2, lon % 2]).astype(jnp.int32).reshape(1, 3)

    grid = np.arange(token_count, dtype=np.int32).reshape(row_count // HALF, HALF, col_count // HALF, HALF)
    halves = grid.transpose(0, 2, 1, 3).reshape(2, half)
    order0 = halves.reshape(2, half // part, part).transpose(1, 0, 2).reshape(token_count)
    gap = np.full(strip, -1, np.int32)
    lead = np.full(edge - strip, -1, np.int32)
    low, high = halves
    order1 = np.concatenate([high[strip:], gap, low[strip:], gap, lead, high[:strip], lead, low[:strip]])
    rows1 = order1.shape[0]
    order0, order1 = jnp.asarray(order0)[None], jnp.asarray(order1)[None]

    shape = jax.ShapeDtypeStruct
    chunks = 2 if local > 1 else 1
    piece_shapes = [shape((rows, channels), BF16) for rows in piece_sizes(pieces_count, slots, chunks)]
    attention_scratch = [
        pltpu.VMEM((token_count, 3 * channels), BF16), pltpu.VMEM((token_count, channels), BF16),
    ]

    layer = 0
    mixed, info, *pieces = call(
        functools.partial(first_kernel, layer=layer, pair_experts=pair_experts),
        [(place, SCALARS), (temper, SCALARS), (tokens.reshape(token_count, channels), ()),
         (order0, ()), (ids, (layer,)),
         (norm_gain, (layer,)), (weight_qkv, (layer,)), (weight_proj, (layer,)), (router, (layer,))],
        [shape((token_count, channels), BF16), shape((token_count, 2), F32)] + piece_shapes,
        attention_scratch,
        flops=4_000_000_000,
    )
    columns1, row1, wqkv1, wproj1 = call(
        functools.partial(ahead_kernel, layer=1, pair_experts=pair_experts),
        [(place, SCALARS), (ids, (1,)), (order1, ()), (weight_qkv, UNREAD), (weight_proj, UNREAD), (info, IN_VMEM)],
        [shape((rows1, 2), F32), shape((1, rows1), F32),
         pltpu.VMEM((channels, 3 * channels), BF16), pltpu.VMEM((channels, channels), BF16)],
        [pltpu.SemaphoreType.DMA((2,))],
        flops=2_000_000_000,
    )
    produced = moe(pieces, pieces_count, weight_in, weight_out, far_in, far_out, layer)
    north, own, corner, east = call(
        combine_kernel,
        [(mixed, IN_VMEM), (info, IN_VMEM), (row1, IN_VMEM)] + [(p, IN_VMEM) for p in produced],
        [shape((half, channels), BF16)] * 2 + [shape((edge, channels), BF16)] * 2,
        flops=1_000_000_000,
    )

    layer = 1
    north = shift(north, -1, 0)
    east = shift(east, 0, -1)
    corner = shift(corner, -1, -1)
    low, high, low_edge, high_edge = call(
        functools.partial(shifted_kernel, layer=layer),
        [(place, SCALARS), (temper, SCALARS), (own, IN_VMEM), (north, IN_VMEM), (east, IN_VMEM), (corner, IN_VMEM),
         (norm_gain, (layer,)), (wqkv1, IN_VMEM), (wproj1, IN_VMEM)],
        [shape((half, channels), BF16)] * 2 + [shape((edge, channels), BF16)] * 2,
        [pltpu.VMEM((half + edge, channels), F32)] * 2 + attention_scratch,
        flops=3_000_000_000,
    )
    high = shift(high, 1, 0)
    low_edge = shift(low_edge, 0, 1)
    high_edge = shift(high_edge, 1, 1)
    mixed, info, *pieces = call(
        route_kernel,
        [(low, IN_VMEM), (high, IN_VMEM), (low_edge, IN_VMEM), (high_edge, IN_VMEM), (columns1, IN_VMEM),
         (row1, IN_VMEM), (norm_gain, (layer,)), (router, (layer,))],
        [shape((rows1, channels), BF16), shape((rows1, 2), F32)] + piece_shapes,
        flops=1_000_000_000,
    )
    produced = moe(pieces, pieces_count, weight_in, weight_out, far_in, far_out, layer)
    (out,) = call(
        last_kernel,
        [(mixed, IN_VMEM), (info, IN_VMEM), (order1, ())] + [(p, IN_VMEM) for p in produced],
        [shape((token_count, channels), BF16)],
        flops=1_000_000_000,
    )
    return out.reshape(row_count, col_count, channels)


def after(value, done):
    return lax.optimization_barrier((value, done))[0]


def in_chunks(count, k):
    return k == 0 or k >= count // 2


def piece_sizes(count, slots, chunks):
    return [n for k in range(count) for n in ([slots // chunks] * chunks if in_chunks(count, k) else [slots])]


def moe(flat, count, own_in, own_out, far_in, far_out, layer):
    local = own_in.shape[1]
    if local > 1:
        half = local // 2
        turns = [
            ([own_in, own_out], [(0, entry, entry // 2) for entry in range(local)], 0),
            ([far_in, far_out], [(0, entry, half + entry // 2) for entry in range(local)], half),
        ]
    else:
        turns = [([own_in, own_out, far_in, far_out], [(0, 0, 0), (1, 0, 0)], 0)]
    rest = iter(flat)
    pieces = [[next(rest) for _ in turns] if in_chunks(count, k) else next(rest) for k in range(count)]
    away = [k for k in range(1, count) if in_chunks(count, k)]
    beside = [k for k in range(1, count) if not in_chunks(count, k)]
    own, held, arrived, whole = [], [], [], None
    for turn, (weights, plan, base) in enumerate(turns):
        sent = [pieces[k][turn] for k in away]
        if own:
            sent = [after(value, own[-1]) for value in sent]
        arrived.append([between(value, 2 * k) for k, value in zip(away, sent)])
        if whole is None:
            whole = [between(pieces[k], 2 * k) for k in beside]
        piece = pieces[0][turn]
        if own:
            piece = after((piece, sent), own[-1])[0]
        out, weights_here = run_near(piece, weights, plan, base, layer)
        own.append(out)
        held.append(weights_here)
    back = {k: [] for k in away}
    kept = []
    for turn, (_, plan, base) in enumerate(turns):
        outs = run_away(whole, arrived[turn], held[turn], plan, base, kept)
        kept = outs[: len(whole)]
        for k, value in zip(away, outs[len(whole) :]):
            if back[k]:
                value = after(value, back[k][-1])
            back[k].append(between(value, 2 * k))
    back[0] = own
    for k, value in zip(beside, kept):
        back[k] = [between(value, 2 * k)]
    return [value for k in range(count) for value in back[k]]


def solution(mesh):
    in_specs = (
        P("lat", "lon", None),
        P(None, "lat", "lon", None, None),
        P(),
        P(),
        P(),
        P(),
        P(),
        P(None, "lon", None, None),
        P(None, "lon", None, None),
    )
    out_specs = P("lat", "lon", None)
    return jax.shard_map(per_device, mesh=mesh, in_specs=in_specs, out_specs=out_specs, check_vma=False)
```
